32 devices in a mesh: seq: 16 (over z, y, core), pool: 2 (over x).
Axes of the slice: x: 2, y: 2, z: 4, core: 2. Of those that a mesh axis runs over, the one named last changes fastest.
Arguments:
- query_rows: bfloat16 [8192, 4096], P('seq', 'pool'), may hold values from -6 to 6
- key_rows: bfloat16 [8192, 4096], P('seq', 'pool'), may hold values from -6 to 6
- value_rows: bfloat16 [8192, 4096], P('seq', 'pool'), may hold values from -6 to 6
- log_decay: float32 [32, 8192], P('pool', 'seq'), may hold values from -0.7 to 0
- residual: bfloat16 [8192, 4096], P(('seq', 'pool')), may hold values from -6 to 6
- out_weight: bfloat16 [4096, 4096], P('pool', 'seq'), may hold values from -0.09375 to 0.09375
- norm_gain: float32 [4096], replicated, may hold values from 0.5 to 1.5
- kv_weight: bfloat16 [4096, 1024], P('seq'), may hold values from -0.09375 to 0.09375
- block_table: int32 [64, 2], P(('seq', 'pool')), may hold values from 0 to 3, as said below
Outputs:
- page_cache: bfloat16 [16, 2, 4, 128, 1024], P('seq', 'pool')
The draws below stay inside these ranges and needn't reach their ends.
Inputs may be any that keep to these rules, and one draw needn't show every extreme that they name: `block_table`: column 0 is a page's pool device, column 1 its slot there. The pages of one index of seq go to pool devices of that same index, no two to the same device and slot; one pool device receives exactly 4 of them, each other at most 4, and all 2 pages of some device go to that one.
All inputs are finite; a program needn't handle non-finite values.
Results may differ from the reference program's by a relative error of at most 0.0056.
Values may be sent and summed in bfloat16 or wider, within the bound.
No kernel may reach another device: no remote copies, remote signals or barrier semaphores. Data moves between devices by JAX's collectives and lax.ppermute only.
A program may use at most 128 MiB of HBM per device.

```python
import jax
import jax.numpy as jnp
from jax import lax

D = 4096
RETENTION_HEADS = 32
HD = 128
PAGE = 128
BLK = 512
TOK_DEV = 512
PROMPT_TOKENS = 8192
KVW = 1024
PAGES_DEV = 2
SLOTS = 4
NPAGES = 64
N_SEQ = 16
N_POOL = 2


def draw_log_decay(key, part):
    parallel_lanes = jax.random.split(key, 7)
    slow_share = 0.5
    slow_heads = jax.random.uniform(parallel_lanes[0], (RETENTION_HEADS,)) < slow_share
    fast_rate = jnp.exp(jax.random.uniform(parallel_lanes[1], (RETENTION_HEADS,), minval=jnp.log(1.0 / 50.0), maxval=jnp.log(1.0 / 30.0)))
    slow_rate = jnp.exp(jax.random.uniform(parallel_lanes[2], (RETENTION_HEADS,), minval=jnp.log(0.03), maxval=jnp.log(0.25))) / PROMPT_TOKENS
    base_rate = jnp.where(slow_heads, slow_rate, fast_rate)
    block_factor = jnp.exp(jax.random.uniform(parallel_lanes[3], (RETENTION_HEADS, N_SEQ), minval=jnp.log(0.5), maxval=jnp.log(2.0)))
    block_factor = jnp.repeat(block_factor, TOK_DEV, axis=1)
    jitter = jax.random.uniform(parallel_lanes[4], (RETENTION_HEADS, PROMPT_TOKENS), minval=0.5, maxval=1.5)
    decay_speed = base_rate[:, None] * block_factor * jitter
    token_positions = jnp.arange(PROMPT_TOKENS, dtype=jnp.int32)
    spike_locations = jax.random.randint(parallel_lanes[5], (RETENTION_HEADS, 2), 0, PROMPT_TOKENS)
    spike_events = jnp.any(token_positions[None, :, None] == spike_locations[:, None, :], axis=-1)
    spike_keep_mask = jax.random.uniform(parallel_lanes[6], (RETENTION_HEADS, PROMPT_TOKENS), minval=0.5, maxval=0.8)
    return jnp.where(spike_events, jnp.log(spike_keep_mask), -decay_speed).astype(jnp.float32)


def draw_block_table(key, part):
    group_pages = PAGES_DEV * N_POOL

    def one_group(group_key):
        parallel_lanes = jax.random.split(group_key, 6)
        heavy = jax.random.randint(parallel_lanes[0], (), 0, N_POOL)
        source = jax.random.randint(parallel_lanes[1], (), 0, N_POOL)
        page_ids = jnp.arange(group_pages, dtype=jnp.int32)
        shuffled = jax.random.permutation(parallel_lanes[2], group_pages)
        ranking_score = jnp.where(page_ids // PAGES_DEV == source, -1, shuffled)
        ranking = jnp.argsort(jnp.argsort(ranking_score, stable=True), stable=True)
        to_heavy = ranking < SLOTS
        others = (heavy + 1 + jax.random.randint(parallel_lanes[3], (group_pages,), 0, N_POOL - 1)) % N_POOL
        owners = jnp.where(to_heavy, heavy, others).astype(jnp.int32)
        order = jax.random.permutation(parallel_lanes[4], group_pages)
        same_owner = owners[:, None] == owners[None, :]
        earlier = order[None, :] < order[:, None]
        place_rank = jnp.sum(jnp.logical_and(same_owner, earlier).astype(jnp.int32), axis=1)
        shifts = jax.random.randint(parallel_lanes[5], (N_POOL,), 0, SLOTS)
        slot_ids = (place_rank + shifts[owners]) % SLOTS
        return jnp.stack([owners, slot_ids.astype(jnp.int32)], axis=1)
    tables = jax.vmap(one_group)(jax.random.split(key, N_SEQ))
    return tables.reshape(NPAGES, 2).astype(jnp.int32)


def steps_of(stream_key, extent, pieces, least, top_value):
    factor_of = 1.0
    for axis_at, shards_of in pieces:
        draws = jax.random.uniform(jax.random.fold_in(jax.random.fold_in(stream_key, 6), axis_at), (shards_of,), jnp.float32, least / len(pieces), top_value / len(pieces))
        factor_of = factor_of * jnp.repeat(jnp.exp(draws), extent[axis_at] // shards_of).reshape((-1,) + (1,) * (len(extent) - 1 - axis_at))
    return factor_of


def centred(key, extent, width, reach, cuts=(), kind=jnp.bfloat16):
    values = width * jax.random.normal(key, extent, jnp.float32)
    if cuts:
        values = values * steps_of(key, extent, cuts, -0.22, 0.18)
    return jnp.clip(values, -reach, reach).astype(kind)


def setup_inputs(seed: int = 0) -> dict:
    seeds = jax.random.split(jax.random.key(seed), 10)
    query_rows = centred(seeds[0], (PROMPT_TOKENS, RETENTION_HEADS * HD), 1.0, 6.0, ((0, 16), (1, 2)))
    key_rows = centred(seeds[1], (PROMPT_TOKENS, RETENTION_HEADS * HD), 1.0, 6.0, ((0, 16), (1, 2)))
    value_rows = centred(seeds[2], (PROMPT_TOKENS, RETENTION_HEADS * HD), 1.0, 6.0, ((0, 16), (1, 2)))
    log_decay = draw_log_decay(jax.random.fold_in(seeds[9], 71), 0)
    residual = centred(seeds[4], (PROMPT_TOKENS, D), 1.0, 6.0, ((0, 32),))
    out_weight = centred(seeds[5], (RETENTION_HEADS * HD, D), D ** -0.5, 0.09375, ((0, 2), (1, 16)))
    norm_gain = jnp.clip(1.0 + 0.1 * jax.random.normal(seeds[6], (D,), jnp.float32), 0.5, 1.5)
    kv_weight = centred(seeds[7], (D, KVW), D ** -0.5, 0.09375, ((0, 16),))
    block_table = draw_block_table(jax.random.fold_in(seeds[9], 71), 0)
    return {"query_rows": query_rows, "key_rows": key_rows, "value_rows": value_rows, "log_decay": log_decay, "residual": residual, "out_weight": out_weight, "norm_gain": norm_gain, "kv_weight": kv_weight, "block_table": block_table}


def retention(query_rows, key_rows, value_rows, log_decay):
    block_count = PROMPT_TOKENS // BLK

    def split_heads(matrix):
        return matrix.reshape(block_count, BLK, RETENTION_HEADS, HD).transpose(0, 2, 1, 3)
    queries = split_heads(query_rows)
    key_heads = split_heads(key_rows)
    value_heads = split_heads(value_rows)
    decays = log_decay.reshape(RETENTION_HEADS, block_count, BLK).transpose(1, 0, 2)
    lower_mask = jnp.tril(jnp.ones((BLK, BLK), dtype=bool))

    def advance(carried, inputs):
        query_blk, key_blk, value_blk, decay_blk = inputs
        cumulative = jnp.cumsum(decay_blk, axis=1)
        block_total = cumulative[:, -1]
        log_gap = jnp.where(lower_mask[None], cumulative[:, :, None] - cumulative[:, None, :], 0.0)
        products = jnp.einsum('hid,hjd->hij', query_blk.astype(jnp.float32), key_blk.astype(jnp.float32))
        scores = jnp.where(lower_mask[None], products * jnp.exp(log_gap), 0.0).astype(jnp.bfloat16)
        inner = jnp.einsum('hij,hjd->hid', scores.astype(jnp.float32), value_blk.astype(jnp.float32))
        outer = jnp.einsum('hid,hde->hie', query_blk.astype(jnp.float32), carried, precision=lax.Precision.HIGHEST) * jnp.exp(cumulative)[:, :, None]
        weighted = (key_blk.astype(jnp.float32) * jnp.exp(block_total[:, None] - cumulative)[:, :, None]).astype(jnp.bfloat16)
        update = jnp.einsum('hjd,hje->hde', weighted.astype(jnp.float32), value_blk.astype(jnp.float32))
        carried = jnp.exp(block_total)[:, None, None] * carried + update
        return (carried, inner + outer)
    initial = jnp.zeros((RETENTION_HEADS, HD, HD), dtype=jnp.float32)
    _, retained = lax.scan(advance, initial, (queries, key_heads, value_heads, decays))
    scaled = retained * lax.rsqrt(lax.optimization_barrier(jnp.mean(retained * retained, axis=-1, keepdims=True)) + 1e-05)
    return scaled.transpose(0, 2, 1, 3).reshape(PROMPT_TOKENS, RETENTION_HEADS * HD).astype(jnp.bfloat16)

def reference(query_rows, key_rows, value_rows, log_decay, residual, out_weight, norm_gain, kv_weight, block_table):
    mixed = retention(query_rows, key_rows, value_rows, log_decay)

    def finish(pair):
        mixed_blk, resid_blk = pair
        hidden = resid_blk.astype(jnp.float32) + jnp.dot(mixed_blk, out_weight, preferred_element_type=jnp.float32)
        normed = (hidden * lax.rsqrt(lax.optimization_barrier(jnp.mean(hidden * hidden, axis=-1, keepdims=True)) + 1e-05) * norm_gain).astype(jnp.bfloat16)
        return jnp.dot(normed, kv_weight, preferred_element_type=jnp.float32).astype(jnp.bfloat16)
    kv_all = lax.map(finish, (mixed.reshape(N_SEQ, TOK_DEV, RETENTION_HEADS * HD), residual.reshape(N_SEQ, TOK_DEV, D)))
    pages = kv_all.reshape(N_SEQ, TOK_DEV // PAGE, PAGE, KVW)
    table = block_table.reshape(N_SEQ, TOK_DEV // PAGE, 2)
    group = jnp.broadcast_to(jnp.arange(N_SEQ, dtype=jnp.int32)[:, None], (N_SEQ, TOK_DEV // PAGE))
    page_cache = jnp.zeros((N_SEQ, N_POOL, SLOTS, PAGE, KVW), dtype=jnp.bfloat16)
    page_cache = page_cache.at[group, table[..., 0], table[..., 1]].set(pages)
    return page_cache
```

```python
import jax
import jax.numpy as jnp
from jax import lax
from jax.sharding import PartitionSpec as P

HD = 128
PAGE = 128
INNER = 4
BF16 = jnp.bfloat16
F32 = jnp.float32


def hop(value, axis, pairs):
    return lax.ppermute(value, axis, pairs)


def seq_xor(value, seq_count, bits):
    return hop(value, "seq", [(j, j ^ bits) for j in range(seq_count)])


def seq_shift(value, seq_count, planes):
    step = planes * INNER
    pairs = [(j, j + step) for j in range(seq_count) if 0 <= j + step < seq_count]
    return hop(value, "seq", pairs)


def pool_shift(value, pool_count, by):
    return hop(value, "pool", [(i, (i + by) % pool_count) for i in range(pool_count)])


def plane_chain(own, seq_count, plane):
    planes = seq_count // INNER
    up, down = [own], [own]
    for _ in range(planes - 1):
        up.append(seq_shift(up[-1], seq_count, 1))
        down.append(seq_shift(down[-1], seq_count, -1))
    blocks = [own]
    for d in range(1, planes):
        blocks.append(jnp.where(plane >= d, up[d], down[planes - d]))
    return blocks


def gathered_totals(totals, seq_count, place, plane):
    planes = seq_count // INNER
    near = jnp.stack([totals] + [seq_xor(totals, seq_count, r) for r in range(1, INNER)])
    order = place ^ jnp.arange(INNER)
    in_plane = near[order]
    parts = [in_plane] + [
        hop(in_plane, "seq", [(j, (j + d * INNER) % seq_count) for j in range(seq_count)])
        for d in range(1, planes)
    ]
    stacked = jnp.stack(parts)
    return stacked[(plane - jnp.arange(planes)) % planes].reshape(seq_count, -1)


def entering_state(update, totals, seq_count, place, plane):
    planes = seq_count // INNER
    heads = update.shape[0]
    share = heads // INNER
    everyone = gathered_totals(totals, seq_count, place, plane)
    pieces = update.astype(BF16).reshape(INNER, share, HD, HD)

    def piece(at):
        return lax.dynamic_index_in_dim(pieces, at, 0, False)

    got = [piece(place)] + [
        seq_xor(piece(place ^ r), seq_count, r) for r in range(1, INNER)
    ]
    got = jnp.stack(got)
    mine = lax.dynamic_slice_in_dim(everyone, place * share, share, 1)
    here = lax.dynamic_slice_in_dim(mine, plane * INNER, INNER, 0)
    by_plane = mine.reshape(planes, INNER, share).sum(1)
    inner_updates = [
        lax.dynamic_index_in_dim(got, place ^ i, 0, False).astype(F32) for i in range(INNER)
    ]
    within = [jnp.zeros_like(inner_updates[0])]
    for i in range(INNER):
        within.append(jnp.exp(here[i])[:, None, None] * within[-1] + inner_updates[i])
    plane_total = within[-1].astype(BF16)
    prefix = jnp.zeros_like(inner_updates[0])
    gap = jnp.zeros((share,), F32)
    for d in range(1, planes):
        arrived = seq_shift(plane_total, seq_count, d).astype(F32)
        prefix = prefix + jnp.exp(gap)[:, None, None] * arrived
        behind = lax.dynamic_index_in_dim(by_plane, jnp.maximum(plane - d, 0), 0, False)
        gap = gap + behind
    outgoing = []
    decay = jnp.zeros((share,), F32)
    for i in range(INNER):
        outgoing.append(
            (within[i] + jnp.exp(decay)[:, None, None] * prefix).astype(BF16)
        )
        decay = decay + here[i]
    outgoing = jnp.stack(outgoing)

    def leaving(at):
        return lax.dynamic_index_in_dim(outgoing, at, 0, False)

    back = [leaving(place)] + [
        seq_xor(leaving(place ^ r), seq_count, r) for r in range(1, INNER)
    ]
    back = jnp.stack(back)
    return jnp.concatenate(
        [lax.dynamic_index_in_dim(back, place ^ h, 0, False) for h in range(INNER)]
    )


def head_major(matrix, head_count):
    return matrix.reshape(matrix.shape[0], head_count, HD).transpose(1, 0, 2)


def retention(query_rows, key_rows, value_rows, log_decay, seq_count, place, plane):
    rows = query_rows.shape[0]
    head_count = query_rows.shape[1] // HD
    lower_mask = jnp.tril(jnp.ones((rows, rows), dtype=bool))
    query_blk = head_major(query_rows, head_count)
    key_blk = head_major(key_rows, head_count)
    value_blk = head_major(value_rows, head_count)
    cumulative = jnp.cumsum(log_decay, axis=1)
    block_total = cumulative[:, -1]
    weighted = (
        key_blk.astype(F32) * jnp.exp(block_total[:, None] - cumulative)[:, :, None]
    ).astype(BF16)
    update = jnp.einsum("hjd,hje->hde", weighted, value_blk, preferred_element_type=F32)
    carried = entering_state(update, block_total, seq_count, place, plane)
    log_gap = jnp.where(lower_mask[None], cumulative[:, :, None] - cumulative[:, None, :], 0.0)
    products = jnp.einsum("hid,hjd->hij", query_blk, key_blk, preferred_element_type=F32)
    scores = jnp.where(lower_mask[None], products * jnp.exp(log_gap), 0.0).astype(BF16)
    inner = jnp.einsum("hij,hjd->hid", scores, value_blk, preferred_element_type=F32)
    outer = (
        jnp.einsum("hid,hde->hie", query_blk, carried, preferred_element_type=F32)
        * jnp.exp(cumulative)[:, :, None]
    )
    retained = inner + outer
    scaled = retained * lax.rsqrt(jnp.mean(retained * retained, axis=-1, keepdims=True) + 1e-05)
    return scaled.transpose(1, 0, 2).reshape(rows, head_count * HD).astype(BF16)


def on_device(
    query_rows,
    key_rows,
    value_rows,
    log_decay,
    residual,
    out_weight,
    norm_gain,
    kv_weight,
    block_table,
):
    seq_count = lax.axis_size("seq")
    pool_count = lax.axis_size("pool")
    planes = seq_count // INNER
    index = lax.axis_index("seq")
    me = lax.axis_index("pool")
    place = index % INNER
    plane = index // INNER
    width = out_weight.shape[1]
    rows_here = residual.shape[0]
    cache_width = kv_weight.shape[1]
    pages_here = block_table.shape[0]
    slot_count = 2 * pages_here

    columns = []
    for block in plane_chain(out_weight, seq_count, plane):
        other = seq_xor(block, seq_count, 2)
        columns.append([block, seq_xor(block, seq_count, 1), other, seq_xor(other, seq_count, 1)])

    kv_share = kv_weight.shape[0] // pool_count
    kv_own = lax.dynamic_slice_in_dim(kv_weight, me * kv_share, kv_share, 0)
    kv_pair = jnp.stack([kv_own, seq_xor(kv_own, seq_count, 2)])
    kv_blocks = []
    for pair in plane_chain(kv_pair, seq_count, plane):
        shares = jnp.stack([pair] + [pool_shift(pair, pool_count, r) for r in range(1, pool_count)])
        shares = shares[(me - jnp.arange(pool_count)) % pool_count]
        whole = shares.transpose(1, 0, 2, 3).reshape(2, kv_weight.shape[0], cache_width)
        swapped = seq_xor(whole, seq_count, 1)
        kv_blocks += [whole[0], swapped[0], whole[1], swapped[1]]

    table_parts = jnp.stack(
        [block_table] + [pool_shift(block_table, pool_count, r) for r in range(1, pool_count)]
    )

    mixed = retention(
        query_rows, key_rows, value_rows, log_decay, seq_count, place, plane
    )

    def rows_of(at):
        return lax.dynamic_slice_in_dim(mixed, at * rows_here, rows_here, 0)

    mixed_mine = rows_of(me)
    mixed_away = [rows_of((me + r) % pool_count) for r in range(1, pool_count)]
    hidden = []
    gains = []
    for d in range(planes):
        total = jnp.concatenate(
            [jnp.dot(mixed_mine, w, preferred_element_type=F32) for w in columns[d]], axis=1
        )
        for r in range(1, pool_count):
            away = jnp.concatenate(
                [
                    jnp.dot(mixed_away[r - 1], w, preferred_element_type=F32).astype(BF16)
                    for w in columns[d]
                ],
                axis=1,
            )
            total = total + pool_shift(away, pool_count, r).astype(F32)
        origin = ((plane - d) % planes) * INNER
        starts = [(origin + (place ^ bits)) * width for bits in range(INNER)]
        total = total + jnp.concatenate(
            [lax.dynamic_slice_in_dim(residual, s, width, 1) for s in starts], axis=1
        ).astype(F32)
        gains += [lax.dynamic_slice_in_dim(norm_gain, s, width, 0) for s in starts]
        hidden.append(total)
    square = sum(jnp.sum(h * h, axis=-1, keepdims=True) for h in hidden)
    scale = lax.rsqrt(square / (width * seq_count) + 1e-05)
    normed = (jnp.concatenate(hidden, axis=1) * scale * jnp.concatenate(gains)).astype(BF16)
    cache_rows = jnp.dot(
        normed, jnp.concatenate(kv_blocks, axis=0), preferred_element_type=F32
    ).astype(BF16)

    own_pages = cache_rows.reshape(pages_here, PAGE, cache_width)
    page_cache = jnp.zeros((slot_count, PAGE, cache_width), BF16)
    slot_ids = jnp.arange(slot_count, dtype=jnp.int32)
    for r in range(pool_count):
        pages = own_pages if r == 0 else pool_shift(own_pages, pool_count, r)
        for p in range(pages_here):
            entry = table_parts[r, p]
            here = jnp.logical_and(entry[0] == me, entry[1] == slot_ids)
            page_cache = jnp.where(here[:, None, None], pages[p][None], page_cache)
    return page_cache.reshape(1, 1, slot_count, PAGE, cache_width)


def solution(mesh):
    placed = (
        P("seq", "pool"),
        P("seq", "pool"),
        P("seq", "pool"),
        P("pool", "seq"),
        P(("seq", "pool"), None),
        P("pool", "seq"),
        P(),
        P("seq", None),
        P(("seq", "pool"), None),
    )
    return jax.shard_map(
        on_device,
        mesh=mesh,
        in_specs=placed,
        out_specs=P("seq", "pool", None, None, None),
        check_vma=False,
    )
```

```python
import functools

import jax
import jax.numpy as jnp
from jax import lax
from jax.experimental import pallas as pl
from jax.experimental.pallas import tpu as pltpu
from jax.sharding import PartitionSpec as P

HD = 128
PAGE = 128
INNER = 4
TAG = 16
EPS = 1e-05
BF16 = jnp.bfloat16
F32 = jnp.float32
SMEM = pl.BlockSpec(memory_space=pltpu.SMEM)
VMEM = pl.BlockSpec(memory_space=pltpu.VMEM)
LIGHT = pl.CostEstimate(flops=1, bytes_accessed=1, transcendentals=0)


def params(mib):
    return pltpu.CompilerParams(vmem_limit_bytes=mib * 2**20)


def call(body, name, out_shape, args, scratch=(), mib=40):
    return pl.pallas_call(
        body,
        name=name,
        out_shape=out_shape,
        in_specs=[SMEM if a.dtype == jnp.int32 else VMEM for a in args],
        out_specs=jax.tree.map(lambda _: VMEM, out_shape),
        scratch_shapes=list(scratch),
        cost_estimate=LIGHT,
        compiler_params=params(mib),
    )(*args)


def shape(dims, dtype):
    return jax.ShapeDtypeStruct(dims, dtype)


def seq_xor(value, seq_count, bits):
    return lax.ppermute(value, "seq", [(j, j ^ bits) for j in range(seq_count)])


def seq_up(value, seq_count, planes):
    step = planes * INNER
    return lax.ppermute(value, "seq", [(j, j + step) for j in range(seq_count - step)])


def pool_shift(value, pool_count, by):
    return lax.ppermute(value, "pool", [(i, (i + by) % pool_count) for i in range(pool_count)])


def ring_chip(spot, planes):
    if isinstance(spot, int):
        return spot * 2 if spot < planes else (2 * planes - 1 - spot) * 2 + 1
    return jnp.where(spot < planes, spot * 2, (2 * planes - 1 - spot) * 2 + 1)


def ring_step(value, seq_count, by):
    planes = seq_count // INNER
    length = 2 * planes
    pairs = []
    for spot in range(length):
        source, target = ring_chip(spot, planes), ring_chip((spot + by) % length, planes)
        pairs += [(source * 2 + core, target * 2 + core) for core in range(2)]
    return lax.ppermute(value, "seq", pairs)


def column(row):
    return jnp.broadcast_to(row, (8, row.shape[1])).T[:, :1]


def update_kernel(meta, key, value, decay, cumul, *outs):
    *pieces, held = outs
    heads, rows = decay.shape
    share = heads // INNER
    before = lax.broadcasted_iota(jnp.int32, (rows, rows), 0)
    after = lax.broadcasted_iota(jnp.int32, (rows, rows), 1)
    ones = (before <= after).astype(F32)
    total = jnp.dot(
        decay[...], ones, precision=lax.Precision.HIGHEST, preferred_element_type=F32
    )
    cumul[...] = total
    upright = total.T
    term = lax.broadcasted_iota(jnp.int32, (TAG, HD), 0)
    place = meta[0]
    for h in range(heads):
        lane = slice(h * HD, (h + 1) * HD)
        last = total[h : h + 1, rows - 1 : rows]
        weight = jnp.exp(last - upright[:, h : h + 1])
        weighted = (key[:, lane].astype(F32) * weight).astype(BF16)
        update = lax.dot_general(
            weighted, value[:, lane], (((0,), (0,)), ((), ())), preferred_element_type=F32
        )
        high = last.astype(BF16).astype(F32)
        middle = (last - high).astype(BF16).astype(F32)
        low = last - high - middle
        tag = jnp.where(
            term == 0, high, jnp.where(term == 1, middle, jnp.where(term == 2, low, 0.0))
        )
        spot = (h // share) ^ place
        held[spot, h % share, :HD, :] = update.astype(BF16)
        held[spot, h % share, HD:, :] = tag.astype(BF16)
    for r in range(INNER):
        pieces[r][...] = held[r]


def state_of(ref, i):
    return ref[i, :HD, :].astype(F32)


def total_of(ref, i):
    return jnp.sum(ref[i, HD:, :].astype(F32), axis=0, keepdims=True)


def stack_in_order(place, got, held):
    for r in range(INNER):
        held[r] = got[r][...]
    return [held.at[place ^ i] for i in range(INNER)]


def plane_kernel(meta, *refs):
    *got, out, held = refs
    parts = stack_in_order(meta[0], got, held)
    term = lax.broadcasted_iota(jnp.int32, (TAG, HD), 0)
    for i in range(out.shape[0]):
        state = jnp.zeros((HD, HD), F32)
        total = jnp.zeros((1, HD), F32)
        for part in parts:
            one = total_of(part, i)
            state = jnp.exp(one) * state + state_of(part, i)
            total = total + one
        high = total.astype(BF16).astype(F32)
        middle = (total - high).astype(BF16).astype(F32)
        low = total - high - middle
        tag = jnp.where(
            term == 0, high, jnp.where(term == 1, middle, jnp.where(term == 2, low, 0.0))
        )
        out[i, :HD, :] = state.astype(BF16)
        out[i, HD:, :] = tag.astype(BF16)


def entering_kernel(meta, *refs):
    held, leaving = refs[-2:]
    outs = refs[-2 - INNER : -2]
    got = refs[:INNER]
    earlier = refs[INNER : -2 - INNER]
    place = meta[0]
    parts = stack_in_order(place, got, held)
    for i in range(leaving.shape[1]):
        state = jnp.zeros((HD, HD), F32)
        gap = jnp.zeros((1, HD), F32)
        for plane in earlier:
            state = state + jnp.exp(gap) * state_of(plane, i)
            gap = gap + total_of(plane, i)
        for spot, part in enumerate(parts):
            leaving[place ^ spot, i] = state.astype(BF16)
            state = jnp.exp(total_of(part, i)) * state + state_of(part, i)
    for r in range(INNER):
        outs[r][...] = leaving[r]


def inner_kernel(query, key, value, cumul, out):
    rows = query.shape[0]
    half = min(256, rows)
    line = cumul[0]
    upright = column(line)
    lower = lax.broadcasted_iota(jnp.int32, (half, half), 0) >= lax.broadcasted_iota(
        jnp.int32, (half, half), 1
    )
    for at in range(0, rows, half):
        here = pl.ds(at, half)
        total = jnp.zeros((half, HD), F32)
        for start in range(0, at + half, half):
            there = pl.ds(start, half)
            products = lax.dot_general(
                query[here, :], key[there, :], (((1,), (1,)), ((), ())), preferred_element_type=F32
            )
            gap = upright[at : at + half] - line[:, start : start + half]
            if start == at:
                scores = jnp.where(lower, products * jnp.exp(jnp.where(lower, gap, 0.0)), 0.0)
            else:
                scores = products * jnp.exp(gap)
            total = total + jnp.dot(
                scores.astype(BF16), value[there, :], preferred_element_type=F32
            )
        out[here, :] = total


def mixed_kernel(meta, query, inner, cumul, *refs):
    *states, out, held = refs
    pool_count, rows, _ = out.shape
    place, me = meta[0], meta[2]
    source = pl.program_id(0) ^ place
    share = cumul.shape[0]
    for i in range(share):
        lane = slice(i * HD, (i + 1) * HD)
        state = states[0][i]
        for r in range(1, INNER):
            state = jnp.where(source == r, states[r][i], state)
        outer = jnp.dot(query[:, lane], state, preferred_element_type=F32)
        retained = inner[:, lane] + outer * jnp.exp(column(cumul[i]))
        mean = jnp.mean(retained * retained, axis=-1, keepdims=True)
        held[:, lane] = (retained * lax.rsqrt(mean + EPS)).astype(BF16)
    for r in range(pool_count):
        start = pl.multiple_of(lax.rem(me + r, pool_count) * rows, rows)
        out[r] = held[pl.ds(start, rows), :]


def project_kernel(parts, splits, *refs):
    own, other = refs[:2]
    weights = refs[2 : 2 + parts]
    mine, *away = refs[2 + parts :]
    pool_count, rows, depth = own.shape
    for r in list(range(1, pool_count)) + [0]:
        for core, mixed in enumerate((own, other)):
            here = pl.ds(core * rows, rows)
            at = 0
            for start in range(0, parts, splits):
                width = weights[start].shape[1]
                total = None
                for s in range(splits):
                    deep = depth // splits
                    part = jnp.dot(
                        mixed[r, :, s * deep : (s + 1) * deep],
                        weights[start + s][...],
                        preferred_element_type=F32,
                    )
                    total = part if total is None else total + part
                if r == 0:
                    mine[here, at : at + width] = total
                else:
                    away[r - 1][here, at : at + width] = total.astype(BF16)
                at += width


def cache_kernel(first, parts, shares, meta, mine, residual, gain, *refs):
    pool_count = shares
    arrived = refs[: pool_count - 1]
    refs = refs[pool_count - 1 :]
    kv = refs[: parts * pool_count]
    refs = refs[parts * pool_count :]
    if not first:
        old_total, old_square = refs[:2]
        refs = refs[2:]
    total, square, held = refs
    me = meta[2]
    depth = kv[0].shape[0]
    for p in range(parts):
        for r in range(pool_count):
            share = lax.rem(me + pool_count - r, pool_count)
            start = pl.multiple_of(p * depth * pool_count + share * depth, depth)
            held[pl.ds(start, depth), :] = kv[p * pool_count + r][...]
    hidden = mine[...] + residual[...].astype(F32)
    for part in arrived:
        hidden = hidden + part[...].astype(F32)
    squares = jnp.sum(hidden * hidden, axis=-1, keepdims=True)
    scaled = (hidden * gain[...]).astype(BF16)
    product = jnp.dot(scaled, held[...], preferred_element_type=F32)
    if first:
        square[...] = jnp.broadcast_to(squares, square.shape)
        total[...] = product
    else:
        square[...] = old_square[...] + squares
        total[...] = old_total[...] + product


def finish_kernel(features, total, square, total_in, square_in, out):
    rows = out.shape[0]
    mean = (square[:rows, :1] + square_in[:, :1]) / features
    out[...] = ((total[:rows, :] + total_in[...]) * lax.rsqrt(mean + EPS)).astype(BF16)


def place_kernel(meta, tables, *refs):
    *pages, out = refs
    me = meta[2]
    out[...] = jnp.zeros(out.shape, out.dtype)
    for r, part in enumerate(pages):
        for p in range(part.shape[0] // PAGE):
            owner, slot = tables[r, 2 * p], tables[r, 2 * p + 1]

            @pl.when(owner == me)
            def _():
                out[slot] = part[p * PAGE : (p + 1) * PAGE, :]


def entering_states(pieces, meta, seq_count):
    planes = seq_count // INNER
    share = pieces[0].shape[0]
    got = [pieces[0]] + [seq_xor(pieces[r], seq_count, r) for r in range(1, INNER)]
    tagged = (share, HD + TAG, HD)
    plane_total = call(
        plane_kernel,
        "plane_state",
        shape(tagged, BF16),
        [meta, *got],
        [pltpu.VMEM((INNER, *tagged), BF16)],
    )
    earlier = [seq_up(plane_total, seq_count, d) for d in range(1, planes)]
    leaving = call(
        entering_kernel,
        "entering_state",
        [shape((share, HD, HD), BF16)] * INNER,
        [meta, *got, *earlier],
        [pltpu.VMEM((INNER, *tagged), BF16), pltpu.VMEM((INNER, share, HD, HD), BF16)],
    )
    return [leaving[0]] + [seq_xor(leaving[r], seq_count, r) for r in range(1, INNER)]


def retention(query_rows, key_rows, value_rows, log_decay, meta, seq_count, pool_count):
    rows, wide = query_rows.shape
    heads = wide // HD
    share = heads // INNER
    tagged = (share, HD + TAG, HD)
    cumul, *pieces = call(
        update_kernel,
        "update",
        [shape(log_decay.shape, F32)] + [shape(tagged, BF16)] * INNER,
        [meta, key_rows, value_rows, log_decay],
        [pltpu.VMEM((INNER, *tagged), BF16)],
    )
    cumul = cumul.reshape(heads, 1, rows)
    states = entering_states(pieces, meta, seq_count)
    by_head = pl.BlockSpec((rows, HD), lambda h: (0, h))
    inner = pl.pallas_call(
        inner_kernel,
        name="inner",
        grid=(heads,),
        out_shape=shape((rows, wide), F32),
        in_specs=[by_head, by_head, by_head, pl.BlockSpec((1, 1, rows), lambda h: (h, 0, 0))],
        out_specs=by_head,
        cost_estimate=LIGHT,
        compiler_params=params(24),
    )(query_rows, key_rows, value_rows, cumul)
    by_share = pl.BlockSpec((rows, share * HD), lambda g: (0, g))
    return pl.pallas_call(
        mixed_kernel,
        name="mixed",
        grid=(INNER,),
        out_shape=shape((pool_count, rows // pool_count, wide), BF16),
        in_specs=[
            SMEM,
            by_share,
            by_share,
            pl.BlockSpec((share, 1, rows), lambda g: (g, 0, 0)),
            *[VMEM] * INNER,
        ],
        out_specs=pl.BlockSpec(
            (pool_count, rows // pool_count, share * HD), lambda g: (0, 0, g)
        ),
        scratch_shapes=[pltpu.VMEM((rows, share * HD), BF16)],
        cost_estimate=LIGHT,
        compiler_params=params(24),
    )(meta, query_rows, inner, cumul, *states)


def ring(own, seq_count):
    length = seq_count // 2
    groups = [([0], [own])]
    ahead, behind = own, own
    for d in range(1, length // 2):
        ahead, behind = ring_step(ahead, seq_count, 1), ring_step(behind, seq_count, -1)
        groups.append(([d, length - d], [ahead, behind]))
    half = own.shape[0] // 2
    groups.append(
        (
            [length // 2],
            [ring_step(ahead[:half], seq_count, 1), ring_step(behind[half:], seq_count, -1)],
        )
    )
    return groups


def on_device(
    query_rows,
    key_rows,
    value_rows,
    log_decay,
    residual,
    out_weight,
    norm_gain,
    kv_weight,
    block_table,
):
    seq_count = lax.axis_size("seq")
    pool_count = lax.axis_size("pool")
    planes = seq_count // INNER
    length = 2 * planes
    index = lax.axis_index("seq")
    me = lax.axis_index("pool")
    place = index % INNER
    plane = index // INNER
    core = index % 2
    spot = jnp.where(place < 2, plane, length - 1 - plane)
    meta = jnp.stack([place, plane, me]).astype(jnp.int32)
    width = out_weight.shape[1]
    rows_here = residual.shape[0]
    cache_width = kv_weight.shape[1]
    pages_here = block_table.shape[0]
    slot_count = 2 * pages_here
    chip_rows = 2 * rows_here

    weight_groups = ring(out_weight, seq_count)
    kv_share = kv_weight.shape[0] // pool_count
    kv_own = lax.dynamic_slice_in_dim(kv_weight, me * kv_share, kv_share, 0)
    kv_groups = []
    for distances, blocks in ring(kv_own, seq_count):
        if len(blocks) > len(distances):
            blocks = [jnp.concatenate(blocks)]
        kv_groups.append(
            [[b] + [pool_shift(b, pool_count, r) for r in range(1, pool_count)] for b in blocks]
        )
    tables = jnp.stack(
        [block_table] + [pool_shift(block_table, pool_count, r) for r in range(1, pool_count)]
    ).reshape(pool_count, 2 * pages_here)
    residual_pair = [residual, seq_xor(residual, seq_count, 1)]

    mixed = retention(
        query_rows, key_rows, value_rows, log_decay, meta, seq_count, pool_count
    )
    mixed_other = seq_xor(mixed, seq_count, 1)

    total = square = None
    for (distances, blocks), kv_parts in zip(weight_groups, kv_groups):
        count = len(distances)
        splits = len(blocks) // count
        wide = count * width
        mine, *away = call(
            functools.partial(project_kernel, len(blocks), splits),
            "project",
            [shape((chip_rows, wide), F32)] + [shape((chip_rows, wide), BF16)] * (pool_count - 1),
            [mixed, mixed_other, *blocks],
        )
        arrived = [pool_shift(away[r - 1], pool_count, r) for r in range(1, pool_count)]
        starts = [
            (ring_chip((spot + length - d) % length, planes) * 2 + core) * width
            for d in distances
        ]
        residual_part = jnp.concatenate(
            [
                jnp.concatenate([lax.dynamic_slice_in_dim(rows, s, width, 1) for s in starts], 1)
                for rows in residual_pair
            ]
        )
        gain_part = jnp.concatenate(
            [lax.dynamic_slice_in_dim(norm_gain, s, width, 0) for s in starts]
        ).reshape(1, wide)
        first = total is None
        total, square = call(
            functools.partial(cache_kernel, first, count, pool_count),
            "cache",
            [shape((chip_rows, cache_width), F32), shape((chip_rows, HD), F32)],
            [meta, mine, residual_part, gain_part, *arrived]
            + [piece for part in kv_parts for piece in part]
            + ([] if first else [total, square]),
            [pltpu.VMEM((wide, cache_width), BF16)],
        )
    features = width * seq_count
    cache_rows = call(
        functools.partial(finish_kernel, features),
        "finish",
        shape((rows_here, cache_width), BF16),
        [
            total,
            square,
            seq_xor(total[rows_here:], seq_count, 1),
            seq_xor(square[rows_here:], seq_count, 1),
        ],
    )
    pages = [cache_rows] + [pool_shift(cache_rows, pool_count, r) for r in range(1, pool_count)]
    page_cache = call(
        place_kernel,
        "place",
        shape((slot_count, PAGE, cache_width), BF16),
        [meta, tables, *pages],
    )
    return page_cache.reshape(1, 1, slot_count, PAGE, cache_width)


def solution(mesh):
    placed = (
        P("seq", "pool"),
        P("seq", "pool"),
        P("seq", "pool"),
        P("pool", "seq"),
        P(("seq", "pool"), None),
        P("pool", "seq"),
        P(),
        P("seq", None),
        P(("seq", "pool"), None),
    )
    return jax.shard_map(
        on_device,
        mesh=mesh,
        in_specs=placed,
        out_specs=P("seq", "pool", None, None, None),
        check_vma=False,
    )
```

```python
import functools

import jax
import jax.numpy as jnp
from jax import lax
from jax.experimental import pallas as pl
from jax.experimental.pallas import tpu as pltpu
from jax.sharding import PartitionSpec as P

HD = 128
PAGE = 128
INNER = 4
TAG = 16
EPS = 1e-05
BF16 = jnp.bfloat16
F32 = jnp.float32
SMEM = pl.BlockSpec(memory_space=pltpu.SMEM)
VMEM = pl.BlockSpec(memory_space=pltpu.VMEM)
FAR = pl.BlockSpec(memory_space=pltpu.HBM)
LIGHT = pl.CostEstimate(flops=1, bytes_accessed=1, transcendentals=0)


def params(mib):
    return pltpu.CompilerParams(vmem_limit_bytes=mib * 2**20)


def call(body, name, out_shape, args, scratch=(), mib=8, far=()):
    return pl.pallas_call(
        body,
        name=name,
        out_shape=out_shape,
        in_specs=[
            SMEM if a.dtype == jnp.int32 else FAR if n in far else VMEM
            for n, a in enumerate(args)
        ],
        out_specs=jax.tree.map(lambda _: VMEM, out_shape),
        scratch_shapes=list(scratch),
        cost_estimate=LIGHT,
        compiler_params=params(mib),
    )(*[in_hbm(a) if n in far else a for n, a in enumerate(args)])


def after(value, *first):
    return lax.optimization_barrier((value, *first))[0]


def in_hbm(value):
    return pltpu.with_memory_space_constraint(value, pltpu.HBM)


def shape(dims, dtype):
    return jax.ShapeDtypeStruct(dims, dtype)


def seq_xor(value, seq_count, bits):
    return lax.ppermute(value, "seq", [(j, j ^ bits) for j in range(seq_count)])


def seq_up(value, seq_count, planes):
    step = planes * INNER
    return lax.ppermute(value, "seq", [(j, j + step) for j in range(seq_count - step)])


def pool_shift(value, pool_count, by):
    return lax.ppermute(value, "pool", [(i, (i + by) % pool_count) for i in range(pool_count)])


def ring_chip(spot, planes):
    if isinstance(spot, int):
        return spot * 2 if spot < planes else (2 * planes - 1 - spot) * 2 + 1
    return jnp.where(spot < planes, spot * 2, (2 * planes - 1 - spot) * 2 + 1)


def ring_step(value, seq_count):
    planes = seq_count // INNER
    length = 2 * planes
    pairs = []
    for spot in range(length):
        for core, by in ((0, 1), (1, -1)):
            source, target = ring_chip(spot, planes), ring_chip((spot + by) % length, planes)
            pairs.append((source * 2 + core, target * 2 + core))
    return lax.ppermute(value, "seq", pairs)


def columns(lines):
    repeat = -(-8 // lines.shape[0])
    return jnp.concatenate([lines] * repeat).T


def tag_of(total):
    term = lax.broadcasted_iota(jnp.int32, (TAG, HD), 0)
    high = total.astype(BF16).astype(F32)
    middle = (total - high).astype(BF16).astype(F32)
    low = total - high - middle
    terms = jnp.where(
        term == 0, high, jnp.where(term == 1, middle, jnp.where(term == 2, low, 0.0))
    )
    return terms.astype(BF16)


def update_kernel(meta, key, value, decay, cumul, *outs):
    *pieces, held = outs
    _, share, rows = cumul.shape
    step = pl.program_id(0)

    @pl.when(step == 0)
    def _():
        before = lax.broadcasted_iota(jnp.int32, (rows, rows), 0)
        upto = lax.broadcasted_iota(jnp.int32, (rows, rows), 1)
        ones = (before <= upto).astype(F32)
        total = jnp.dot(
            decay[...], ones, precision=lax.Precision.HIGHEST, preferred_element_type=F32
        )
        for n in range(INNER):
            cumul[n] = total[n * share : (n + 1) * share]

    lines = cumul[step]
    weights = columns(jnp.exp(lines[:, rows - 1 :] - lines))
    for i in range(share):
        lane = slice(i * HD, (i + 1) * HD)
        weighted = (key[:, lane].astype(F32) * weights[:, i : i + 1]).astype(BF16)
        update = lax.dot_general(
            weighted, value[:, lane], (((0,), (0,)), ((), ())), preferred_element_type=F32
        )
        spot = step ^ meta[0]
        held[spot, i, :HD, :] = update.astype(BF16)
        held[spot, i, HD:, :] = tag_of(lines[i : i + 1, rows - 1 :])

    @pl.when(step == INNER - 1)
    def _():
        for r in range(INNER):
            pieces[r][...] = held[r]


def state_of(ref, i):
    return ref[i, :HD, :].astype(F32)


def total_of(ref, i):
    return jnp.sum(ref[i, HD:, :].astype(F32), axis=0, keepdims=True)


def stack_in_order(place, got, held):
    for r in range(INNER):
        held[r] = got[r][...]
    return [held.at[place ^ i] for i in range(INNER)]


def plane_kernel(meta, *refs):
    *got, out, held = refs
    parts = stack_in_order(meta[0], got, held)
    for i in range(out.shape[0]):
        state = jnp.zeros((HD, HD), F32)
        total = jnp.zeros((1, HD), F32)
        for part in parts:
            one = total_of(part, i)
            state = jnp.exp(one) * state + state_of(part, i)
            total = total + one
        out[i, :HD, :] = state.astype(BF16)
        out[i, HD:, :] = tag_of(total)


def entering_kernel(meta, *refs):
    held, leaving = refs[-2:]
    outs = refs[-2 - INNER : -2]
    got = refs[:INNER]
    earlier = refs[INNER : -2 - INNER]
    place = meta[0]
    parts = stack_in_order(place, got, held)
    for i in range(leaving.shape[1]):
        state = jnp.zeros((HD, HD), F32)
        gap = jnp.zeros((1, HD), F32)
        for plane in earlier:
            state = state + jnp.exp(gap) * state_of(plane, i)
            gap = gap + total_of(plane, i)
        for spot, part in enumerate(parts):
            leaving[place ^ spot, i] = state.astype(BF16)
            state = jnp.exp(total_of(part, i)) * state + state_of(part, i)
    for r in range(INNER):
        outs[r][...] = leaving[r]


def inner_kernel(query, key, value, cumul, out):
    rows = query.shape[0]
    half = min(256, rows)
    lines = cumul[0]
    upright = columns(lines)
    row = lax.broadcasted_iota(jnp.int32, (half, half), 0)
    col = lax.broadcasted_iota(jnp.int32, (half, half), 1)
    bar = jnp.where(row >= col, 0.0, -1e30)
    for i in range(lines.shape[0]):
        lane = slice(i * HD, (i + 1) * HD)
        for at in range(0, rows, half):
            here = slice(at, at + half)
            total = None
            for start in range(0, at + half, half):
                there = slice(start, start + half)
                products = lax.dot_general(
                    query[here, lane],
                    key[there, lane],
                    (((1,), (1,)), ((), ())),
                    preferred_element_type=F32,
                )
                gap = upright[here, i : i + 1] - lines[i : i + 1, there]
                if start == at:
                    gap = gap + bar
                scores = (products * jnp.exp(gap)).astype(BF16)
                part = jnp.dot(scores, value[there, lane], preferred_element_type=F32)
                total = part if total is None else total + part
            out[here, lane] = total


def mixed_kernel(meta, query, *refs):
    inners = refs[:2]
    cumul, *refs = refs[2:]
    *states, out, held = refs
    pool_count, rows, _ = out.shape
    step = pl.program_id(0)
    place, me = meta[0], meta[2]
    lines = cumul[0]
    grown = columns(jnp.exp(lines))
    for i in range(lines.shape[0]):
        lane = slice(i * HD, (i + 1) * HD)
        state = states[0][i]
        for r in range(1, INNER):
            state = jnp.where(step ^ place == r, states[r][i], state)
        outer = jnp.dot(query[:, lane], state, preferred_element_type=F32)
        held[:, lane] = outer * grown[:, i : i + 1]
    for n in range(INNER):

        @pl.when(step == n)
        def _():
            part = n % (INNER // 2) * held.shape[1]
            held[...] = held[...] + inners[n // (INNER // 2)][:, part : part + held.shape[1]]

    for r in range(pool_count):
        start = pl.multiple_of(lax.rem(me + r, pool_count) * rows, rows)
        for i in range(lines.shape[0]):
            lane = slice(i * HD, (i + 1) * HD)
            retained = held[pl.ds(start, rows), lane]
            mean = jnp.mean(retained * retained, axis=-1, keepdims=True)
            out[r, :, lane] = (retained * lax.rsqrt(mean + EPS)).astype(BF16)


def pack_kernel(weight, kv, out):
    depth, width = weight.shape
    rows = kv.shape[0]
    out[:depth, :] = weight[...]
    for c in range(kv.shape[1] // width):
        here = slice(c * width, (c + 1) * width)
        out[depth + c * rows : depth + (c + 1) * rows, :] = kv[:, here]


def project_kernel(joins, parts, *refs):
    if joins:
        own, other = refs[:2]
        both = refs[-1]
        refs = refs[2:-1]
        rows = own.shape[1]
        both[:, :rows, :] = own[...]
        both[:, rows:, :] = other[...]
    else:
        both = refs[0]
        refs = refs[1:]
    blocks = refs[:parts]
    kv, mine, *away = refs[parts:]
    pool_count, _, depth = both.shape
    width = blocks[0].shape[1]
    rows = kv.shape[0] // parts
    for r in list(range(1, pool_count)) + [0]:
        for p in range(parts):
            here = slice(p * width, (p + 1) * width)
            total = jnp.dot(both[r], blocks[p][:depth, :], preferred_element_type=F32)
            if r == 0:
                mine[:, here] = total
            else:
                away[r - 1][:, here] = total.astype(BF16)
    for p in range(parts):
        for c in range(kv.shape[1] // width):
            below = slice(depth + c * rows, depth + (c + 1) * rows)
            kv[p * rows : (p + 1) * rows, c * width : (c + 1) * width] = blocks[p][below, :]


def cache_kernel(first, parts, width, at, meta, mine, *refs):
    own_rows, other_rows, kv, gain, *refs = refs
    *arrived, scaled, near, sems = refs
    arrived, sums = arrived[:-4], arrived[-4:]
    if not first:
        arrived, old = arrived[:-4], arrived[-4:]
    rows = own_rows.shape[0]
    whole = own_rows.shape[1] == parts * width
    copies = []
    for p in range(parts if not whole else 0):
        here = slice(p * width, (p + 1) * width)
        there = pl.ds(pl.multiple_of(meta[at + p], width), width)
        for n, source in enumerate((own_rows, other_rows)):
            target = near.at[n * rows : (n + 1) * rows, here]
            copies.append(
                pltpu.make_async_copy(source.at[:, there], target, sems.at[2 * p + n])
            )
            copies[-1].start()
    for copy in copies:
        copy.wait()
    if whole:
        near[:rows, :] = own_rows[...]
        near[rows:, :] = other_rows[...]
    squares = 0.0
    for p in range(parts):
        here = slice(p * width, (p + 1) * width)
        there = here if whole else pl.ds(pl.multiple_of(meta[at + p], width), width)
        values = near[:, here].astype(F32) + mine[:, here]
        for part in arrived:
            values = values + part[:, here].astype(F32)
        squares = squares + jnp.sum(values * values, axis=-1, keepdims=True)
        scaled[:, here] = (values * gain[:, there]).astype(BF16)
    for n in range(2):
        here = slice(n * rows, (n + 1) * rows)
        product = jnp.dot(scaled[here, :], kv[...], preferred_element_type=F32)
        if first:
            sums[n][...] = product
            sums[2 + n][...] = jnp.broadcast_to(squares[here], (rows, HD))
        else:
            sums[n][...] = old[n][...] + product
            sums[2 + n][...] = old[2 + n][...] + squares[here]


def finish_kernel(features, total, square, total_in, square_in, out):
    mean = (square[:, :1] + square_in[:, :1]) / features
    out[...] = ((total[...] + total_in[...]) * lax.rsqrt(mean + EPS)).astype(BF16)


def place_kernel(pool_count, meta, *refs):
    tables = refs[:pool_count]
    *pages, out = refs[pool_count:]
    me = meta[2]
    out[...] = jnp.zeros(out.shape, out.dtype)
    for table, part in zip(tables, pages):
        for p in range(part.shape[0] // PAGE):
            owner, slot = table[p, 0], table[p, 1]

            @pl.when(owner == me)
            def _():
                out[slot] = part[p * PAGE : (p + 1) * PAGE, :]


def inner_part(n, count, query_rows, key_rows, value_rows, cumul):
    rows = query_rows.shape[0]
    _, share, _ = cumul.shape
    there = pl.BlockSpec((rows, share * HD), lambda i: (0, i + n))
    return pl.pallas_call(
        inner_kernel,
        name="inner",
        grid=(count,),
        out_shape=shape((rows, count * share * HD), F32),
        in_specs=[there] * 3 + [pl.BlockSpec((1, share, rows), lambda i: (i + n, 0, 0))],
        out_specs=pl.BlockSpec((rows, share * HD), lambda i: (0, i)),
        cost_estimate=LIGHT,
        compiler_params=params(12),
    )(in_hbm(query_rows), in_hbm(key_rows), in_hbm(value_rows), cumul)


def on_device(
    query_rows,
    key_rows,
    value_rows,
    log_decay,
    residual,
    out_weight,
    norm_gain,
    kv_weight,
    block_table,
):
    seq_count = lax.axis_size("seq")
    pool_count = lax.axis_size("pool")
    planes = seq_count // INNER
    length = 2 * planes
    index = lax.axis_index("seq")
    me = lax.axis_index("pool")
    place = index % INNER
    plane = index // INNER
    core = index % 2
    spot = jnp.where(place < 2, plane, length - 1 - plane)
    width = out_weight.shape[1]
    steps = length // 2
    starts = []
    for g in range(steps + 1):
        chip = ring_chip((spot + length + jnp.where(core == 0, -g, g)) % length, planes)
        cores = [core] if g in (0, steps) else [core, 1 - core]
        starts.append([(chip * 2 + c) * width for c in cores])
    meta = jnp.stack([place, plane, me] + sum(starts, [])).astype(jnp.int32)
    rows, wide = query_rows.shape
    heads = wide // HD
    share = heads // INNER
    rows_here = residual.shape[0]
    cache_width = kv_weight.shape[1]
    pages_here = block_table.shape[0]
    slot_count = 2 * pages_here
    chip_rows = 2 * rows_here
    tagged = (share, HD + TAG, HD)

    packed = shape(
        (out_weight.shape[0] + kv_weight.shape[0] * cache_width // width, width), BF16
    )
    weights = call(pack_kernel, "pack", packed, [out_weight, kv_weight])
    last = 2 * steps - 1
    come = {-1: weights, 0: seq_xor(weights, seq_count, 1)}

    def serve(n, *first):
        come[n] = ring_step(after(come[n - 2], *first) if first else come[n - 2], seq_count)
        return come[n]

    def arrivals(g):
        if g == 0:
            return [come[-1]]
        if g == steps:
            return [come[last]]
        return [come[2 * g - 1], come[2 * g]]

    serve(1)
    tables = [block_table] + [pool_shift(block_table, pool_count, r) for r in range(1, pool_count)]
    residual_other = seq_xor(residual, seq_count, 1)

    by_share = pl.BlockSpec((rows, share * HD), lambda g: (0, g))
    cumul, *pieces = pl.pallas_call(
        update_kernel,
        name="update",
        grid=(INNER,),
        out_shape=[shape((INNER, share, rows), F32)] + [shape(tagged, BF16)] * INNER,
        in_specs=[SMEM, by_share, by_share, pl.BlockSpec((heads, rows), lambda g: (0, 0))],
        out_specs=[pl.BlockSpec((INNER, share, rows), lambda g: (0, 0, 0))]
        + [pl.BlockSpec(tagged, lambda g: (0, 0, 0))] * INNER,
        scratch_shapes=[pltpu.VMEM((INNER, *tagged), BF16)],
        cost_estimate=LIGHT,
        compiler_params=params(12),
    )(meta, in_hbm(key_rows), in_hbm(value_rows), log_decay)
    pieces[1] = after(pieces[1], residual_other, *tables)
    got = [pieces[0]] + [seq_xor(pieces[r], seq_count, r) for r in range(1, INNER)]

    inners = [inner_part(0, INNER // 2, query_rows, key_rows, value_rows, cumul)]
    serve(2, got[1])
    got[1] = after(got[1], inners[0])
    plane_total = call(
        plane_kernel,
        "plane_state",
        shape(tagged, BF16),
        [meta, *got],
        [pltpu.VMEM((INNER, *tagged), BF16)],
    )
    earlier = [seq_up(plane_total, seq_count, d) for d in range(1, planes)]
    inners.append(
        inner_part(
            INNER // 2, INNER // 2, after(query_rows, plane_total), key_rows, value_rows, cumul
        )
    )
    serve(3, earlier[0])
    earlier[1] = after(earlier[1], inners[1], come[1], come[2])
    leaving = call(
        entering_kernel,
        "entering_state",
        [shape((share, HD, HD), BF16)] * INNER,
        [meta, *got, *earlier],
        [pltpu.VMEM((INNER, *tagged), BF16), pltpu.VMEM((INNER, share, HD, HD), BF16)],
    )
    states = [leaving[0]] + [seq_xor(leaving[r], seq_count, r) for r in range(1, INNER)]
    serve(4, states[1])
    states[2] = after(states[2], come[3])

    mixed = pl.pallas_call(
        mixed_kernel,
        name="mixed",
        grid=(INNER,),
        out_shape=shape((pool_count, rows_here, wide), BF16),
        in_specs=[SMEM, by_share]
        + [VMEM] * 2
        + [pl.BlockSpec((1, share, rows), lambda g: (g, 0, 0))]
        + [VMEM] * INNER,
        out_specs=pl.BlockSpec((pool_count, rows_here, share * HD), lambda g: (0, 0, g)),
        scratch_shapes=[pltpu.VMEM((rows, share * HD), F32)],
        cost_estimate=LIGHT,
        compiler_params=params(12),
    )(meta, in_hbm(query_rows), *inners, cumul, *states)
    mixed_other = seq_xor(mixed, seq_count, 1)
    serve(5, mixed)
    both = []

    def project(g, *first):
        blocks = arrivals(g)
        count = len(blocks)
        out_wide = count * width
        joins = not both
        sources = [after(both[0], *first)] if both else [mixed, mixed_other]
        joined = [shape((pool_count, chip_rows, wide), BF16)] if joins else []
        kv, mine, *away = call(
            functools.partial(project_kernel, joins, count),
            "project",
            [shape((out_wide, cache_width), BF16), shape((chip_rows, out_wide), F32)]
            + [shape((chip_rows, out_wide), BF16)] * (pool_count - 1)
            + joined,
            [*sources, *blocks],
            mib=12,
        )
        if joins:
            both.append(away.pop())
        arrived = [pool_shift(away[r - 1], pool_count, r) for r in range(1, pool_count)]
        return mine, kv, arrived

    def cache(g, projected, sums, *first):
        mine, kv, arrived = projected
        count = len(starts[g])
        out_wide = count * width
        around = [residual, residual_other, norm_gain.reshape(1, -1)]
        if width % HD:
            around = [
                jnp.concatenate([lax.dynamic_slice_in_dim(a, s, width, 1) for s in starts[g]], 1)
                for a in around
            ]
        return call(
            functools.partial(
                cache_kernel, not sums, count, width, 3 + sum(len(x) for x in starts[:g])
            ),
            "cache",
            [shape((rows_here, cache_width), F32)] * 2 + [shape((rows_here, HD), F32)] * 2,
            [
                meta,
                after(mine, *first),
                *around[:2],
                kv,
                around[2],
                *arrived,
                *sums,
            ],
            [
                pltpu.VMEM((chip_rows, out_wide), BF16),
                pltpu.VMEM((chip_rows, out_wide), BF16),
                pltpu.SemaphoreType.DMA((2 * count,)),
            ],
            mib=12,
            far=() if width % HD else (2, 3),
        )

    projected = {0: project(0)}
    done = (projected[0][0],)
    sums = ()
    cached = 0

    def reduce_one():
        nonlocal sums, done, cached
        sums = cache(cached, projected[cached], sums, *done)
        done = (sums[2],)
        cached += 1

    for g in range(1, steps + 1):
        if g >= 2:
            for n in (2 * g - 1, 2 * g):
                if n <= last:
                    if 5 < n + 2 <= last:
                        serve(n + 2, come[n], *done)
                    done = (*done, come[n])
        projected[g] = project(g, *done)
        done = (projected[g][0],)
        if 2 <= g < steps:
            reduce_one()
    while cached <= steps:
        reduce_one()
    own_total, other_total, own_square, other_square = sums
    cache_rows = call(
        functools.partial(finish_kernel, width * seq_count),
        "finish",
        shape((rows_here, cache_width), BF16),
        [
            own_total,
            own_square,
            seq_xor(other_total, seq_count, 1),
            seq_xor(other_square, seq_count, 1),
        ],
    )
    pages = [cache_rows] + [pool_shift(cache_rows, pool_count, r) for r in range(1, pool_count)]
    page_cache = call(
        functools.partial(place_kernel, pool_count),
        "place",
        shape((slot_count, PAGE, cache_width), BF16),
        [meta, *tables, *pages],
    )
    return page_cache.reshape(1, 1, slot_count, PAGE, cache_width)


def solution(mesh):
    placed = (
        P("seq", "pool"),
        P("seq", "pool"),
        P("seq", "pool"),
        P("pool", "seq"),
        P(("seq", "pool"), None),
        P("pool", "seq"),
        P(),
        P("seq", None),
        P(("seq", "pool"), None),
    )
    return jax.shard_map(
        on_device,
        mesh=mesh,
        in_specs=placed,
        out_specs=P("seq", "pool", None, None, None),
        check_vma=False,
    )
```

```python
import functools

import jax
import jax.numpy as jnp
from jax import lax
from jax.experimental import pallas as pl
from jax.experimental.pallas import tpu as pltpu
from jax.sharding import PartitionSpec as P

HD = 128
PAGE = 128
INNER = 4
TAG = 16
EPS = 1e-05
BF16 = jnp.bfloat16
F32 = jnp.float32
SMEM = pl.BlockSpec(memory_space=pltpu.SMEM)
VMEM = pl.BlockSpec(memory_space=pltpu.VMEM)
FAR = pl.BlockSpec(memory_space=pltpu.HBM)
LIGHT = pl.CostEstimate(flops=1, bytes_accessed=1, transcendentals=0)


def params(mib):
    return pltpu.CompilerParams(vmem_limit_bytes=mib * 2**20)


def call(body, name, out_shape, args, scratch=(), mib=8, far=()):
    return pl.pallas_call(
        body,
        name=name,
        out_shape=out_shape,
        in_specs=[
            SMEM if a.dtype == jnp.int32 else FAR if n in far else VMEM
            for n, a in enumerate(args)
        ],
        out_specs=jax.tree.map(lambda _: VMEM, out_shape),
        scratch_shapes=list(scratch),
        cost_estimate=LIGHT,
        compiler_params=params(mib),
    )(*[in_hbm(a) if n in far else a for n, a in enumerate(args)])


def after(value, *first):
    return lax.optimization_barrier((value, *first))[0]


def in_hbm(value):
    return pltpu.with_memory_space_constraint(value, pltpu.HBM)


def shape(dims, dtype):
    return jax.ShapeDtypeStruct(dims, dtype)


def seq_xor(value, seq_count, bits):
    return lax.ppermute(value, "seq", [(j, j ^ bits) for j in range(seq_count)])


def seq_index(plane, row, core):
    return plane * INNER + row * 2 + core


def to_other_row(value, seq_count, first_plane):
    pairs = []
    for plane in range(first_plane, seq_count // INNER):
        for row in range(2):
            core = row if plane == 0 else 1 - row
            pairs.append((seq_index(plane, row, core), seq_index(plane, 1 - row, row)))
    return lax.ppermute(value, "seq", pairs)


def to_later_planes(value, seq_count, reach):
    planes = seq_count // INNER
    return [
        lax.ppermute(
            value,
            "seq",
            [
                (seq_index(plane, row, 1 - row), seq_index(plane + by, row, 1 - row))
                for plane in range(reach - 1, planes - by, 2 * reach)
                for row in range(2)
            ],
        )
        for by in range(1, reach + 1)
    ]


def pool_shift(value, pool_count, by):
    return lax.ppermute(value, "pool", [(i, (i + by) % pool_count) for i in range(pool_count)])


def ring_chip(spot, planes):
    if isinstance(spot, int):
        return spot * 2 if spot < planes else (2 * planes - 1 - spot) * 2 + 1
    return jnp.where(spot < planes, spot * 2, (2 * planes - 1 - spot) * 2 + 1)


def ring_step(value, seq_count):
    planes = seq_count // INNER
    length = 2 * planes
    pairs = []
    for spot in range(length):
        for core, by in ((0, 1), (1, -1)):
            source, target = ring_chip(spot, planes), ring_chip((spot + by) % length, planes)
            pairs.append((source * 2 + core, target * 2 + core))
    return lax.ppermute(value, "seq", pairs)


def columns(lines):
    repeat = -(-8 // lines.shape[0])
    return jnp.concatenate([lines] * repeat).T


def tag_of(total):
    term = lax.broadcasted_iota(jnp.int32, (TAG, HD), 0)
    high = total.astype(BF16).astype(F32)
    middle = (total - high).astype(BF16).astype(F32)
    low = total - high - middle
    terms = jnp.where(
        term == 0, high, jnp.where(term == 1, middle, jnp.where(term == 2, low, 0.0))
    )
    return terms.astype(BF16)


def update_kernel(key, value, decay, cumul, out):
    _, share, rows = cumul.shape
    step = pl.program_id(0)

    @pl.when(step == 0)
    def _():
        before = lax.broadcasted_iota(jnp.int32, (rows, rows), 0)
        upto = lax.broadcasted_iota(jnp.int32, (rows, rows), 1)
        ones = (before <= upto).astype(F32)
        total = jnp.dot(
            decay[...], ones, precision=lax.Precision.HIGHEST, preferred_element_type=F32
        )
        for n in range(INNER):
            cumul[n] = total[n * share : (n + 1) * share]

    lines = cumul[step]
    weights = columns(jnp.exp(lines[:, rows - 1 :] - lines))
    for i in range(share):
        lane = slice(i * HD, (i + 1) * HD)
        weighted = (key[:, lane].astype(F32) * weights[:, i : i + 1]).astype(BF16)
        update = lax.dot_general(
            weighted, value[:, lane], (((0,), (0,)), ((), ())), preferred_element_type=F32
        )
        out[i, :HD, :] = update.astype(BF16)
        out[i, HD:, :] = tag_of(lines[i : i + 1, rows - 1 :])


def state_of(ref, i):
    return ref[i, :HD, :].astype(F32)


def total_of(ref, i):
    return jnp.sum(ref[i, HD:, :].astype(F32), axis=0, keepdims=True)


def either(choice, one, two, i):
    state = jnp.where(choice, state_of(one, i), state_of(two, i))
    return state, jnp.where(choice, total_of(one, i), total_of(two, i))


def chip_kernel(meta, own, other, out):
    lead = meta[0] % 2 == 0
    for i in range(out.shape[0]):
        state, total = either(lead, own, other, i)
        after_state, after_total = either(lead, other, own, i)
        out[i, :HD, :] = (jnp.exp(after_total) * state + after_state).astype(BF16)
        out[i, HD:, :] = tag_of(total + after_total)


def plane_kernel(meta, own, other, out):
    row = meta[0] // 2
    for i in range(out.shape[0]):
        h = row * out.shape[0] + i
        state, total = either(row == 0, own, other, h)
        after_state, after_total = either(row == 0, other, own, h)
        out[i, :HD, :] = (jnp.exp(after_total) * state + after_state).astype(BF16)
        out[i, HD:, :] = tag_of(total + after_total)


def scan_kernel(reach, meta, *refs):
    received, refs = refs[:reach], refs[reach:]
    if reach > 1:
        before, *refs = refs
    own, *outs = refs
    upper = meta[1] // reach % 2 == 1
    by = meta[1] % reach
    for i in range(own.shape[0]):
        state, total = state_of(received[0], i), total_of(received[0], i)
        for n in range(1, reach):
            state = jnp.where(by == n, state_of(received[n], i), state)
            total = jnp.where(by == n, total_of(received[n], i), total)
        state = jnp.where(upper, state, 0.0)
        total = jnp.where(upper, total, 0.0)
        if reach > 1:
            later = total_of(before, i)
            state = jnp.exp(later) * state + state_of(before, i)
            total = total + later
        outs[0][i, :HD, :] = state.astype(BF16)
        outs[0][i, HD:, :] = tag_of(total)
        if len(outs) > 1:
            later = total_of(own, i)
            outs[1][i, :HD, :] = (jnp.exp(later) * state + state_of(own, i)).astype(BF16)
            outs[1][i, HD:, :] = tag_of(total + later)


def start_kernel(meta, own, other, row_update, prefix, other_prefix, mine, away):
    row, lead = meta[0] // 2, meta[0] % 2 == 0
    half = prefix.shape[0]
    for i in range(mine.shape[0]):
        here = row == i // half
        state = jnp.where(here, state_of(prefix, i % half), state_of(other_prefix, i % half))
        grown = jnp.exp(total_of(row_update, i)) * state + state_of(row_update, i)
        state = jnp.where(row == 0, state, grown)
        update, total = either(lead, own, other, i)
        later = jnp.exp(total) * state + update
        mine[i] = jnp.where(lead, state, later).astype(BF16)
        away[i] = jnp.where(lead, later, state).astype(BF16)


def inner_kernel(query, key, value, cumul, out):
    rows = query.shape[0]
    half = min(256, rows)
    lines = cumul[0]
    upright = columns(lines)
    row = lax.broadcasted_iota(jnp.int32, (half, half), 0)
    col = lax.broadcasted_iota(jnp.int32, (half, half), 1)
    bar = jnp.where(row >= col, 0.0, -1e30)
    for i in range(lines.shape[0]):
        lane = slice(i * HD, (i + 1) * HD)
        for at in range(0, rows, half):
            here = slice(at, at + half)
            total = None
            for start in range(0, at + half, half):
                there = slice(start, start + half)
                products = lax.dot_general(
                    query[here, lane],
                    key[there, lane],
                    (((1,), (1,)), ((), ())),
                    preferred_element_type=F32,
                )
                gap = upright[here, i : i + 1] - lines[i : i + 1, there]
                if start == at:
                    gap = gap + bar
                scores = (products * jnp.exp(gap)).astype(BF16)
                part = jnp.dot(scores, value[there, lane], preferred_element_type=F32)
                total = part if total is None else total + part
            out[here, lane] = total


def mixed_kernel(meta, query, *refs):
    inners = refs[:3]
    cumul, *refs = refs[3:]
    own_state, other_state, *outs, held = refs
    pool_count, rows = len(outs), outs[0].shape[0]
    step = pl.program_id(0)
    gathers = meta[0] // 2 + meta[0] % 2 == 1
    me = meta[2]
    lines = cumul[0]
    grown = columns(jnp.exp(lines))
    for i in range(lines.shape[0]):
        lane = slice(i * HD, (i + 1) * HD)
        state = jnp.where(gathers, own_state[i], other_state[i])
        outer = jnp.dot(query[:, lane], state, preferred_element_type=F32)
        held[:, lane] = outer * grown[:, i : i + 1]
    for n in range(INNER):

        @pl.when(step == n)
        def _():
            part = (n if n < 2 else 0) * held.shape[1]
            held[...] = held[...] + inners[max(0, n - 1)][:, part : part + held.shape[1]]

    for r in range(pool_count):
        start = pl.multiple_of(lax.rem(me + r, pool_count) * rows, rows)
        for i in range(lines.shape[0]):
            lane = slice(i * HD, (i + 1) * HD)
            retained = held[pl.ds(start, rows), lane]
            mean = jnp.mean(retained * retained, axis=-1, keepdims=True)
            outs[r][:, lane] = (retained * lax.rsqrt(mean + EPS)).astype(BF16)


def pack_kernel(weight, kv, out):
    depth, width = weight.shape
    rows = kv.shape[0]
    out[:depth, :] = weight[...]
    for c in range(kv.shape[1] // width):
        here = slice(c * width, (c + 1) * width)
        out[depth + c * rows : depth + (c + 1) * rows, :] = kv[:, here]


def project_kernel(joins, parts, *refs):
    if joins:
        both = refs[-1]
        rows = refs[0].shape[0]
        for r in range(joins):
            both[r, :rows, :] = refs[r][...]
            both[r, rows:, :] = refs[joins + r][...]
        refs = refs[2 * joins : -1]
    else:
        both = refs[0]
        refs = refs[1:]
    blocks = refs[:parts]
    kv, mine, *away = refs[parts:]
    pool_count, _, depth = both.shape
    width = blocks[0].shape[1]
    rows = kv.shape[0] // parts
    for r in list(range(1, pool_count)) + [0]:
        for p in range(parts):
            here = slice(p * width, (p + 1) * width)
            total = jnp.dot(both[r], blocks[p][:depth, :], preferred_element_type=F32)
            if r == 0:
                mine[:, here] = total
            else:
                away[r - 1][:, here] = total.astype(BF16)
    for p in range(parts):
        for c in range(kv.shape[1] // width):
            below = slice(depth + c * rows, depth + (c + 1) * rows)
            kv[p * rows : (p + 1) * rows, c * width : (c + 1) * width] = blocks[p][below, :]


def cache_kernel(first, parts, width, at, meta, mine, *refs):
    own_rows, other_rows, kv, gain, *refs = refs
    *arrived, scaled, near, sems = refs
    arrived, sums = arrived[:-4], arrived[-4:]
    if not first:
        arrived, old = arrived[:-4], arrived[-4:]
    rows = own_rows.shape[0]
    whole = own_rows.shape[1] == parts * width
    copies = []
    for p in range(parts if not whole else 0):
        here = slice(p * width, (p + 1) * width)
        there = pl.ds(pl.multiple_of(meta[at + p], width), width)
        for n, source in enumerate((own_rows, other_rows)):
            target = near.at[n * rows : (n + 1) * rows, here]
            copies.append(
                pltpu.make_async_copy(source.at[:, there], target, sems.at[2 * p + n])
            )
            copies[-1].start()
    for copy in copies:
        copy.wait()
    if whole:
        near[:rows, :] = own_rows[...]
        near[rows:, :] = other_rows[...]
    squares = 0.0
    for p in range(parts):
        here = slice(p * width, (p + 1) * width)
        there = here if whole else pl.ds(pl.multiple_of(meta[at + p], width), width)
        values = near[:, here].astype(F32) + mine[:, here]
        for part in arrived:
            values = values + part[:, here].astype(F32)
        squares = squares + jnp.sum(values * values, axis=-1, keepdims=True)
        scaled[:, here] = (values * gain[:, there]).astype(BF16)
    for n in range(2):
        here = slice(n * rows, (n + 1) * rows)
        product = jnp.dot(scaled[here, :], kv[...], preferred_element_type=F32)
        if first:
            sums[n][...] = product
            sums[2 + n][...] = jnp.broadcast_to(squares[here], (rows, HD))
        else:
            sums[n][...] = old[n][...] + product
            sums[2 + n][...] = old[2 + n][...] + squares[here]


def finish_kernel(features, total, square, total_in, square_in, out):
    mean = (square[:, :1] + square_in[:, :1]) / features
    out[...] = ((total[...] + total_in[...]) * lax.rsqrt(mean + EPS)).astype(BF16)


def place_kernel(pool_count, meta, *refs):
    tables = refs[:pool_count]
    *pages, out = refs[pool_count:]
    me = meta[2]
    out[...] = jnp.zeros(out.shape, out.dtype)
    for table, part in zip(tables, pages):
        for p in range(part.shape[0] // PAGE):
            owner, slot = table[p, 0], table[p, 1]

            @pl.when(owner == me)
            def _():
                out[slot] = part[p * PAGE : (p + 1) * PAGE, :]


def inner_part(n, count, query_rows, key_rows, value_rows, cumul):
    rows = query_rows.shape[0]
    _, share, _ = cumul.shape
    there = pl.BlockSpec((rows, share * HD), lambda i: (0, i + n))
    return pl.pallas_call(
        inner_kernel,
        name="inner",
        grid=(count,),
        out_shape=shape((rows, count * share * HD), F32),
        in_specs=[there] * 3 + [pl.BlockSpec((1, share, rows), lambda i: (i + n, 0, 0))],
        out_specs=pl.BlockSpec((rows, share * HD), lambda i: (0, i)),
        cost_estimate=LIGHT,
        compiler_params=params(12),
    )(in_hbm(query_rows), in_hbm(key_rows), in_hbm(value_rows), cumul)


def on_device(
    query_rows,
    key_rows,
    value_rows,
    log_decay,
    residual,
    out_weight,
    norm_gain,
    kv_weight,
    block_table,
):
    seq_count = lax.axis_size("seq")
    pool_count = lax.axis_size("pool")
    planes = seq_count // INNER
    length = 2 * planes
    index = lax.axis_index("seq")
    me = lax.axis_index("pool")
    place = index % INNER
    plane = index // INNER
    core = index % 2
    spot = jnp.where(place < 2, plane, length - 1 - plane)
    width = out_weight.shape[1]
    steps = length // 2
    starts = []
    for g in range(steps + 1):
        chip = ring_chip((spot + length + jnp.where(core == 0, -g, g)) % length, planes)
        cores = [core] if g in (0, steps) else [core, 1 - core]
        starts.append([(chip * 2 + c) * width for c in cores])
    meta = jnp.stack([place, plane, me] + sum(starts, [])).astype(jnp.int32)
    rows, wide = query_rows.shape
    heads = wide // HD
    share = heads // INNER
    rows_here = residual.shape[0]
    cache_width = kv_weight.shape[1]
    pages_here = block_table.shape[0]
    slot_count = 2 * pages_here
    chip_rows = 2 * rows_here

    packed = shape(
        (out_weight.shape[0] + kv_weight.shape[0] * cache_width // width, width), BF16
    )
    weights = call(pack_kernel, "pack", packed, [out_weight, kv_weight])
    last = 2 * steps - 1
    come = {-1: weights, 0: seq_xor(weights, seq_count, 1)}

    def serve(n, *first):
        come[n] = ring_step(after(come[n - 2], *first) if first else come[n - 2], seq_count)
        return come[n]

    def arrivals(g):
        if g == 0:
            return [come[-1]]
        if g == steps:
            return [come[last]]
        return [come[2 * g - 1], come[2 * g]]

    serve(1)
    by_share = pl.BlockSpec((rows, share * HD), lambda g: (0, g))
    cumul, update = pl.pallas_call(
        update_kernel,
        name="update",
        grid=(INNER,),
        out_shape=[shape((INNER, share, rows), F32), shape((heads, HD + TAG, HD), BF16)],
        in_specs=[by_share, by_share, pl.BlockSpec((heads, rows), lambda g: (0, 0))],
        out_specs=[
            pl.BlockSpec((INNER, share, rows), lambda g: (0, 0, 0)),
            pl.BlockSpec((share, HD + TAG, HD), lambda g: (g, 0, 0)),
        ],
        cost_estimate=LIGHT,
        compiler_params=params(12),
    )(in_hbm(key_rows), in_hbm(value_rows), log_decay)
    update = after(update, come[0])
    update_other = seq_xor(update, seq_count, 1)
    serve(2, update_other)
    chip = call(
        chip_kernel, "chip_state", shape(update.shape, BF16), [meta, update, update_other]
    )
    chip_other = to_other_row(chip, seq_count, 0)
    inners = [inner_part(0, INNER // 2, query_rows, key_rows, value_rows, cumul)]
    chip_other = after(chip_other, inners[0], come[1])
    tagged = (heads // 2, HD + TAG, HD)
    plane_update = call(plane_kernel, "plane_state", shape(tagged, BF16), [meta, chip, chip_other])
    serve(3, plane_update)
    table = after(block_table, plane_update)
    tables = [block_table] + [pool_shift(table, pool_count, r) for r in range(1, pool_count)]
    total = plane_update
    before = []
    reach = 1
    while reach < planes:
        received = to_later_planes(total, seq_count, reach)
        if len(inners) < 3:
            query = after(query_rows, total)
            inners.append(
                inner_part(1 + len(inners), 1, query, key_rows, value_rows, cumul)
            )
            first = (come[2], *tables) if reach == 1 else (come[3],)
            received[0] = after(received[0], inners[-1], *first)
        final = 2 * reach >= planes
        prefix, *rest = call(
            functools.partial(scan_kernel, reach),
            "scan_state",
            [shape(tagged, BF16)] * (1 if final else 2),
            [meta, *received, *before, plane_update],
        )
        if reach == 1:
            serve(4, prefix)
        before, total = [prefix], (rest or [None])[0]
        reach *= 2
    prefix_other = to_other_row(prefix, seq_count, 1)
    residual_other = seq_xor(after(residual, prefix), seq_count, 1)
    serve(5, prefix)
    own_state, away_state = call(
        start_kernel,
        "start_state",
        [shape((heads, HD, HD), BF16)] * 2,
        [meta, update, update_other, chip_other, prefix, prefix_other],
    )
    other_state = after(seq_xor(away_state, seq_count, 1), come[4])

    mixed = pl.pallas_call(
        mixed_kernel,
        name="mixed",
        grid=(INNER,),
        out_shape=[shape((rows_here, wide), BF16)] * pool_count,
        in_specs=[SMEM, by_share]
        + [VMEM] * 3
        + [pl.BlockSpec((1, share, rows), lambda g: (g, 0, 0))]
        + [pl.BlockSpec((share, HD, HD), lambda g: (g, 0, 0))] * 2,
        out_specs=[pl.BlockSpec((rows_here, share * HD), lambda g: (0, g))] * pool_count,
        scratch_shapes=[pltpu.VMEM((rows, share * HD), F32)],
        cost_estimate=LIGHT,
        compiler_params=params(12),
    )(meta, in_hbm(query_rows), *inners, cumul, own_state, other_state)
    mixed_other = [seq_xor(part, seq_count, 1) for part in mixed]
    serve(6, mixed[0])
    both = []

    def project(g, *first):
        blocks = arrivals(g)
        count = len(blocks)
        out_wide = count * width
        joins = not both
        sources = [after(both[0], *first)] if both else [*mixed, *mixed_other]
        joined = [shape((pool_count, chip_rows, wide), BF16)] if joins else []
        kv, mine, *away = call(
            functools.partial(project_kernel, pool_count if joins else 0, count),
            "project",
            [shape((out_wide, cache_width), BF16), shape((chip_rows, out_wide), F32)]
            + [shape((chip_rows, out_wide), BF16)] * (pool_count - 1)
            + joined,
            [*sources, *blocks],
            mib=12,
        )
        if joins:
            both.append(away.pop())
        arrived = [pool_shift(away[r - 1], pool_count, r) for r in range(1, pool_count)]
        return mine, kv, arrived

    def cache(g, projected, sums, *first):
        mine, kv, arrived = projected
        count = len(starts[g])
        out_wide = count * width
        around = [residual, residual_other, norm_gain.reshape(1, -1)]
        if width % HD:
            around = [
                jnp.concatenate([lax.dynamic_slice_in_dim(a, s, width, 1) for s in starts[g]], 1)
                for a in around
            ]
        return call(
            functools.partial(
                cache_kernel, not sums, count, width, 3 + sum(len(x) for x in starts[:g])
            ),
            "cache",
            [shape((rows_here, cache_width), F32)] * 2 + [shape((rows_here, HD), F32)] * 2,
            [
                meta,
                after(mine, *first),
                *around[:2],
                kv,
                around[2],
                *arrived,
                *sums,
            ],
            [
                pltpu.VMEM((chip_rows, out_wide), BF16),
                pltpu.VMEM((chip_rows, out_wide), BF16),
                pltpu.SemaphoreType.DMA((2 * count,)),
            ],
            mib=12,
            far=() if width % HD else (2, 3),
        )

    projected = {0: project(0)}
    done = (projected[0][0],)
    sums = ()
    cached = 0

    def reduce_one():
        nonlocal sums, done, cached
        sums = cache(cached, projected[cached], sums, *done)
        done = (sums[2],)
        cached += 1

    for g in range(1, steps + 1):
        if g > 2:
            done = (*done, *[come[m] for m in (2 * g - 1, 2 * g) if m <= last])
        projected[g] = project(g, *done)
        done = (projected[g][0],)
        if g == 1:
            continue
        if g == 2:
            done = (*done, residual_other)
            reduce_one()
        for n in (2 * g + 3, 2 * g + 4):
            if n not in come and n <= last:
                serve(n, come[n - 2], *done)
                done = (*done, come[n - 2])
        while g < steps and cached <= g - 1:
            reduce_one()
    while cached <= steps:
        reduce_one()
    own_total, other_total, own_square, other_square = sums
    cache_rows = call(
        functools.partial(finish_kernel, width * seq_count),
        "finish",
        shape((rows_here, cache_width), BF16),
        [
            own_total,
            own_square,
            seq_xor(other_total, seq_count, 1),
            seq_xor(other_square, seq_count, 1),
        ],
    )
    pages = [cache_rows] + [pool_shift(cache_rows, pool_count, r) for r in range(1, pool_count)]
    page_cache = call(
        functools.partial(place_kernel, pool_count),
        "place",
        shape((slot_count, PAGE, cache_width), BF16),
        [meta, *tables, *pages],
    )
    return page_cache.reshape(1, 1, slot_count, PAGE, cache_width)


def solution(mesh):
    placed = (
        P("seq", "pool"),
        P("seq", "pool"),
        P("seq", "pool"),
        P("pool", "seq"),
        P(("seq", "pool"), None),
        P("pool", "seq"),
        P(),
        P("seq", None),
        P(("seq", "pool"), None),
    )
    return jax.shard_map(
        on_device,
        mesh=mesh,
        in_specs=placed,
        out_specs=P("seq", "pool", None, None, None),
        check_vma=False,
    )
```

```python
import functools

import jax
import jax.numpy as jnp
from jax import lax
from jax.experimental import pallas as pl
from jax.experimental.pallas import tpu as pltpu
from jax.sharding import PartitionSpec as P

HD = 128
PAGE = 128
INNER = 4
TAG = 16
EPS = 1e-05
BF16 = jnp.bfloat16
F32 = jnp.float32
SMEM = pl.BlockSpec(memory_space=pltpu.SMEM)
VMEM = pl.BlockSpec(memory_space=pltpu.VMEM)
FAR = pl.BlockSpec(memory_space=pltpu.HBM)
LIGHT = pl.CostEstimate(flops=1, bytes_accessed=1, transcendentals=0)


def params(mib):
    return pltpu.CompilerParams(vmem_limit_bytes=mib * 2**20)


def call(body, name, out_shape, args, scratch=(), mib=8, far=()):
    return pl.pallas_call(
        body,
        name=name,
        out_shape=out_shape,
        in_specs=[
            SMEM if a.dtype == jnp.int32 else FAR if n in far else VMEM
            for n, a in enumerate(args)
        ],
        out_specs=jax.tree.map(lambda _: VMEM, out_shape),
        scratch_shapes=list(scratch),
        cost_estimate=LIGHT,
        compiler_params=params(mib),
    )(*[in_hbm(a) if n in far else a for n, a in enumerate(args)])


def after(value, *first):
    return lax.optimization_barrier((value, *first))[0]


def in_hbm(value):
    return pltpu.with_memory_space_constraint(value, pltpu.HBM)


def shape(dims, dtype):
    return jax.ShapeDtypeStruct(dims, dtype)


def seq_xor(value, seq_count, bits):
    return lax.ppermute(value, "seq", [(j, j ^ bits) for j in range(seq_count)])


def seq_index(plane, row, core):
    return plane * INNER + row * 2 + core


def to_other_row(value, seq_count, first_plane):
    pairs = []
    for plane in range(first_plane, seq_count // INNER):
        for row in range(2):
            core = row if plane == 0 else 1 - row
            pairs.append((seq_index(plane, row, core), seq_index(plane, 1 - row, row)))
    return lax.ppermute(value, "seq", pairs)


def to_later_planes(value, seq_count, reach):
    planes = seq_count // INNER
    return [
        lax.ppermute(
            value,
            "seq",
            [
                (seq_index(plane, row, 1 - row), seq_index(plane + by, row, 1 - row))
                for plane in range(reach - 1, planes - by, 2 * reach)
                for row in range(2)
            ],
        )
        for by in range(1, reach + 1)
    ]


def pool_shift(value, pool_count, by):
    return lax.ppermute(value, "pool", [(i, (i + by) % pool_count) for i in range(pool_count)])


def ring_chip(spot, planes):
    if isinstance(spot, int):
        return spot * 2 if spot < planes else (2 * planes - 1 - spot) * 2 + 1
    return jnp.where(spot < planes, spot * 2, (2 * planes - 1 - spot) * 2 + 1)


def ring_step(value, seq_count):
    planes = seq_count // INNER
    length = 2 * planes
    pairs = []
    for spot in range(length):
        for core, by in ((0, 1), (1, -1)):
            source, target = ring_chip(spot, planes), ring_chip((spot + by) % length, planes)
            pairs.append((source * 2 + core, target * 2 + core))
    return lax.ppermute(value, "seq", pairs)


def columns(lines):
    repeat = -(-8 // lines.shape[0])
    return jnp.concatenate([lines] * repeat).T


def tag_of(total):
    term = lax.broadcasted_iota(jnp.int32, (TAG, HD), 0)
    high = total.astype(BF16).astype(F32)
    middle = (total - high).astype(BF16).astype(F32)
    low = total - high - middle
    terms = jnp.where(
        term == 0, high, jnp.where(term == 1, middle, jnp.where(term == 2, low, 0.0))
    )
    return terms.astype(BF16)


def update_kernel(key, value, decay, cumul, out):
    _, share, rows = cumul.shape
    step = pl.program_id(0)

    @pl.when(step == 0)
    def _():
        before = lax.broadcasted_iota(jnp.int32, (rows, rows), 0)
        upto = lax.broadcasted_iota(jnp.int32, (rows, rows), 1)
        ones = (before <= upto).astype(F32)
        total = jnp.dot(
            decay[...], ones, precision=lax.Precision.HIGHEST, preferred_element_type=F32
        )
        for n in range(INNER):
            cumul[n] = total[n * share : (n + 1) * share]

    lines = cumul[step]
    weights = columns(jnp.exp(lines[:, rows - 1 :] - lines))
    for i in range(share):
        lane = slice(i * HD, (i + 1) * HD)
        weighted = (key[:, lane].astype(F32) * weights[:, i : i + 1]).astype(BF16)
        update = lax.dot_general(
            weighted, value[:, lane], (((0,), (0,)), ((), ())), preferred_element_type=F32
        )
        out[i, :HD, :] = update.astype(BF16)
        out[i, HD:, :] = tag_of(lines[i : i + 1, rows - 1 :])


def state_of(ref, i):
    return ref[i, :HD, :].astype(F32)


def total_of(ref, i):
    return jnp.sum(ref[i, HD:, :].astype(F32), axis=0, keepdims=True)


def either(choice, one, two, i):
    state = jnp.where(choice, state_of(one, i), state_of(two, i))
    return state, jnp.where(choice, total_of(one, i), total_of(two, i))


def chip_kernel(meta, own, other, out):
    lead = meta[0] % 2 == 0
    for i in range(out.shape[0]):
        state, total = either(lead, own, other, i)
        after_state, after_total = either(lead, other, own, i)
        out[i, :HD, :] = (jnp.exp(after_total) * state + after_state).astype(BF16)
        out[i, HD:, :] = tag_of(total + after_total)


def plane_kernel(meta, own, other, out):
    row = meta[0] // 2
    for i in range(out.shape[0]):
        h = row * out.shape[0] + i
        state, total = either(row == 0, own, other, h)
        after_state, after_total = either(row == 0, other, own, h)
        out[i, :HD, :] = (jnp.exp(after_total) * state + after_state).astype(BF16)
        out[i, HD:, :] = tag_of(total + after_total)


def scan_kernel(reach, meta, *refs):
    received, refs = refs[:reach], refs[reach:]
    if reach > 1:
        before, *refs = refs
    own, *outs = refs
    upper = meta[1] // reach % 2 == 1
    by = meta[1] % reach
    for i in range(own.shape[0]):
        state, total = state_of(received[0], i), total_of(received[0], i)
        for n in range(1, reach):
            state = jnp.where(by == n, state_of(received[n], i), state)
            total = jnp.where(by == n, total_of(received[n], i), total)
        state = jnp.where(upper, state, 0.0)
        total = jnp.where(upper, total, 0.0)
        if reach > 1:
            later = total_of(before, i)
            state = jnp.exp(later) * state + state_of(before, i)
            total = total + later
        outs[0][i, :HD, :] = state.astype(BF16)
        outs[0][i, HD:, :] = tag_of(total)
        if len(outs) > 1:
            later = total_of(own, i)
            outs[1][i, :HD, :] = (jnp.exp(later) * state + state_of(own, i)).astype(BF16)
            outs[1][i, HD:, :] = tag_of(total + later)


def start_kernel(meta, own, other, row_update, prefix, other_prefix, mine, away):
    row, lead = meta[0] // 2, meta[0] % 2 == 0
    half = prefix.shape[0]
    for i in range(mine.shape[0]):
        here = row == i // half
        state = jnp.where(here, state_of(prefix, i % half), state_of(other_prefix, i % half))
        grown = jnp.exp(total_of(row_update, i)) * state + state_of(row_update, i)
        state = jnp.where(row == 0, state, grown)
        update, total = either(lead, own, other, i)
        later = jnp.exp(total) * state + update
        mine[i] = jnp.where(lead, state, later).astype(BF16)
        away[i] = jnp.where(lead, later, state).astype(BF16)


def inner_kernel(query, key, value, cumul, out):
    rows = query.shape[0]
    half = min(256, rows)
    lines = cumul[0]
    upright = columns(lines)
    row = lax.broadcasted_iota(jnp.int32, (half, half), 0)
    col = lax.broadcasted_iota(jnp.int32, (half, half), 1)
    bar = jnp.where(row >= col, 0.0, -1e30)
    for i in range(lines.shape[0]):
        lane = slice(i * HD, (i + 1) * HD)
        for at in range(0, rows, half):
            here = slice(at, at + half)
            total = None
            for start in range(0, at + half, half):
                there = slice(start, start + half)
                products = lax.dot_general(
                    query[here, lane],
                    key[there, lane],
                    (((1,), (1,)), ((), ())),
                    preferred_element_type=F32,
                )
                gap = upright[here, i : i + 1] - lines[i : i + 1, there]
                if start == at:
                    gap = gap + bar
                scores = (products * jnp.exp(gap)).astype(BF16)
                part = jnp.dot(scores, value[there, lane], preferred_element_type=F32)
                total = part if total is None else total + part
            out[here, lane] = total


def mixed_kernel(meta, query, *refs):
    inners = refs[:3]
    cumul, *refs = refs[3:]
    own_state, other_state, *outs, held = refs
    pool_count, rows = len(outs), outs[0].shape[0]
    step = pl.program_id(0)
    gathers = meta[0] // 2 + meta[0] % 2 == 1
    me = meta[2]
    lines = cumul[0]
    grown = columns(jnp.exp(lines))
    for i in range(lines.shape[0]):
        lane = slice(i * HD, (i + 1) * HD)
        state = jnp.where(gathers, own_state[i], other_state[i])
        outer = jnp.dot(query[:, lane], state, preferred_element_type=F32)
        held[:, lane] = outer * grown[:, i : i + 1]
    for n in range(INNER):

        @pl.when(step == n)
        def _():
            part = (n if n < 2 else 0) * held.shape[1]
            held[...] = held[...] + inners[max(0, n - 1)][:, part : part + held.shape[1]]

    for r in range(pool_count):
        start = pl.multiple_of(lax.rem(me + r, pool_count) * rows, rows)
        for i in range(lines.shape[0]):
            lane = slice(i * HD, (i + 1) * HD)
            retained = held[pl.ds(start, rows), lane]
            mean = jnp.mean(retained * retained, axis=-1, keepdims=True)
            outs[r][:, lane] = (retained * lax.rsqrt(mean + EPS)).astype(BF16)


def pack_kernel(weight, kv, out):
    depth, width = weight.shape
    rows = kv.shape[0]
    out[:depth, :] = weight[...]
    for c in range(kv.shape[1] // width):
        here = slice(c * width, (c + 1) * width)
        out[depth + c * rows : depth + (c + 1) * rows, :] = kv[:, here]


def cut_kernel(block, out):
    out[...] = block[block.shape[0] - out.shape[0] :, :]


def widen_kernel(meta, block, *refs):
    *shares, out = refs
    rows = shares[0].shape[0]
    depth = block.shape[0] - rows
    out[:depth, :] = block[:depth, :]
    for r, part in enumerate(shares):
        share = lax.rem(meta[2] + len(shares) - r, len(shares))
        start = pl.multiple_of(depth + share * rows, rows)
        out[pl.ds(start, rows), :] = part[...]


def project_kernel(joins, parts, *refs):
    if joins:
        both = refs[-1]
        rows = refs[0].shape[0]
        for r in range(joins):
            both[r, :rows, :] = refs[r][...]
            both[r, rows:, :] = refs[joins + r][...]
        refs = refs[2 * joins : -1]
    else:
        both = refs[0]
        refs = refs[1:]
    blocks = refs[:parts]
    mine, *away = refs[parts:]
    pool_count, _, depth = both.shape
    width = blocks[0].shape[1]
    for r in list(range(1, pool_count)) + [0]:
        for p in range(parts):
            here = slice(p * width, (p + 1) * width)
            total = jnp.dot(both[r], blocks[p][:depth, :], preferred_element_type=F32)
            if r == 0:
                mine[:, here] = total
            else:
                away[r - 1][:, here] = total.astype(BF16)


def cache_kernel(first, parts, shares, kv_count, width, at, meta, mine, *refs):
    own_rows, other_rows, gain, *refs = refs
    kv, refs = refs[:kv_count], refs[kv_count:]
    *arrived, held, scaled, near, sems = refs
    arrived, sums = arrived[:-4], arrived[-4:]
    if not first:
        arrived, old = arrived[:-4], arrived[-4:]
    rows = own_rows.shape[0]
    whole = own_rows.shape[1] == parts * width
    copies = []
    for p in range(parts if not whole else 0):
        here = slice(p * width, (p + 1) * width)
        there = pl.ds(pl.multiple_of(meta[at + p], width), width)
        for n, source in enumerate((own_rows, other_rows)):
            target = near.at[n * rows : (n + 1) * rows, here]
            copies.append(
                pltpu.make_async_copy(source.at[:, there], target, sems.at[2 * p + n])
            )
            copies[-1].start()
    depth = width // shares
    chunks = held.shape[1] // width
    if kv_count == 1 and parts == 1 and kv[0].shape == held.shape:
        held[...] = kv[0][...]
    else:
        each = kv_count // parts
        for p in range(parts):
            for r in range(shares):
                source = kv[p * each + (r if each > 1 else 0)]
                share = lax.rem(meta[2] + shares - r, shares) if each > 1 else r
                start = p * width + share * depth
                if each > 1:
                    start = pl.multiple_of(start, depth)
                base = source.shape[0] - chunks * depth * (1 if each > 1 else shares - r)
                for c in range(chunks):
                    held[pl.ds(start, depth), c * width : (c + 1) * width] = source[
                        base + c * depth : base + (c + 1) * depth, :
                    ]
    for copy in copies:
        copy.wait()
    if whole:
        near[:rows, :] = own_rows[...]
        near[rows:, :] = other_rows[...]
    squares = 0.0
    for p in range(parts):
        here = slice(p * width, (p + 1) * width)
        there = here if whole else pl.ds(pl.multiple_of(meta[at + p], width), width)
        values = near[:, here].astype(F32) + mine[:, here]
        for part in arrived:
            values = values + part[:, here].astype(F32)
        squares = squares + jnp.sum(values * values, axis=-1, keepdims=True)
        scaled[:, here] = (values * gain[:, there]).astype(BF16)
    for n in range(2):
        here = slice(n * rows, (n + 1) * rows)
        product = jnp.dot(scaled[here, :], held[...], preferred_element_type=F32)
        if first:
            sums[n][...] = product
            sums[2 + n][...] = jnp.broadcast_to(squares[here], (rows, HD))
        else:
            sums[n][...] = old[n][...] + product
            sums[2 + n][...] = old[2 + n][...] + squares[here]


def finish_kernel(features, total, square, total_in, square_in, out):
    mean = (square[:, :1] + square_in[:, :1]) / features
    out[...] = ((total[...] + total_in[...]) * lax.rsqrt(mean + EPS)).astype(BF16)


def place_kernel(pool_count, meta, *refs):
    tables = refs[:pool_count]
    *pages, out = refs[pool_count:]
    me = meta[2]
    out[...] = jnp.zeros(out.shape, out.dtype)
    for table, part in zip(tables, pages):
        for p in range(part.shape[0] // PAGE):
            owner, slot = table[p, 0], table[p, 1]

            @pl.when(owner == me)
            def _():
                out[slot] = part[p * PAGE : (p + 1) * PAGE, :]


def inner_part(n, count, query_rows, key_rows, value_rows, cumul):
    rows = query_rows.shape[0]
    _, share, _ = cumul.shape
    there = pl.BlockSpec((rows, share * HD), lambda i: (0, i + n))
    return pl.pallas_call(
        inner_kernel,
        name="inner",
        grid=(count,),
        out_shape=shape((rows, count * share * HD), F32),
        in_specs=[there] * 3 + [pl.BlockSpec((1, share, rows), lambda i: (i + n, 0, 0))],
        out_specs=pl.BlockSpec((rows, share * HD), lambda i: (0, i)),
        cost_estimate=LIGHT,
        compiler_params=params(12),
    )(in_hbm(query_rows), in_hbm(key_rows), in_hbm(value_rows), cumul)


def on_device(
    query_rows,
    key_rows,
    value_rows,
    log_decay,
    residual,
    out_weight,
    norm_gain,
    kv_weight,
    block_table,
):
    seq_count = lax.axis_size("seq")
    pool_count = lax.axis_size("pool")
    planes = seq_count // INNER
    length = 2 * planes
    index = lax.axis_index("seq")
    me = lax.axis_index("pool")
    place = index % INNER
    plane = index // INNER
    core = index % 2
    spot = jnp.where(place < 2, plane, length - 1 - plane)
    width = out_weight.shape[1]
    steps = length // 2
    starts = []
    for g in range(steps + 1):
        chip = ring_chip((spot + length + jnp.where(core == 0, -g, g)) % length, planes)
        cores = [core] if g in (0, steps) else [core, 1 - core]
        starts.append([(chip * 2 + c) * width for c in cores])
    meta = jnp.stack([place, plane, me] + sum(starts, [])).astype(jnp.int32)
    rows, wide = query_rows.shape
    heads = wide // HD
    share = heads // INNER
    rows_here = residual.shape[0]
    cache_width = kv_weight.shape[1]
    pages_here = block_table.shape[0]
    slot_count = 2 * pages_here
    chip_rows = 2 * rows_here

    kv_share = kv_weight.shape[0] // pool_count
    kv_rows = kv_share * cache_width // width
    kv_own = lax.dynamic_slice_in_dim(kv_weight, me * kv_share, kv_share, 0)
    packed = shape((out_weight.shape[0] + kv_rows, width), BF16)
    weights = call(pack_kernel, "pack", packed, [out_weight, kv_own])
    last = 2 * steps - 1
    come = {-1: weights, 0: seq_xor(weights, seq_count, 1)}
    shares = {}

    def spread(n, *first):
        part = call(
            cut_kernel,
            "cut",
            shape((kv_rows, width), BF16),
            [after(come[n], *first) if first else come[n]],
        )
        shares[n] = [part] + [pool_shift(part, pool_count, r) for r in range(1, pool_count)]
        return shares[n]

    def serve(n, *first):
        block = after(come[n - 2], *first) if first else come[n - 2]
        if n - 2 in (3, 4):
            whole = shape((out_weight.shape[0] + kv_rows * pool_count, width), BF16)
            block = call(widen_kernel, "widen", whole, [meta, block, *shares[n - 2]])
        come[n] = ring_step(block, seq_count)
        return come[n]

    def arrivals(g):
        if g == 0:
            return [come[-1]]
        if g == steps:
            return [come[last]]
        return [come[2 * g - 1], come[2 * g]]

    def kv_of(g):
        if g == 0:
            return [kv_weight]
        if g < 3:
            return [part for n in (2 * g - 1, 2 * g) for part in shares[n]]
        return arrivals(g)

    serve(1)

    by_share = pl.BlockSpec((rows, share * HD), lambda g: (0, g))
    cumul, update = pl.pallas_call(
        update_kernel,
        name="update",
        grid=(INNER,),
        out_shape=[shape((INNER, share, rows), F32), shape((heads, HD + TAG, HD), BF16)],
        in_specs=[by_share, by_share, pl.BlockSpec((heads, rows), lambda g: (0, 0))],
        out_specs=[
            pl.BlockSpec((INNER, share, rows), lambda g: (0, 0, 0)),
            pl.BlockSpec((share, HD + TAG, HD), lambda g: (g, 0, 0)),
        ],
        cost_estimate=LIGHT,
        compiler_params=params(12),
    )(in_hbm(key_rows), in_hbm(value_rows), log_decay)
    update = after(update, come[0])
    update_other = seq_xor(update, seq_count, 1)
    serve(2, update_other)
    chip = call(
        chip_kernel, "chip_state", shape(update.shape, BF16), [meta, update, update_other]
    )
    chip_other = to_other_row(chip, seq_count, 0)
    inners = [inner_part(0, INNER // 2, query_rows, key_rows, value_rows, cumul)]
    chip_other = after(chip_other, inners[0], come[1])
    tagged = (heads // 2, HD + TAG, HD)
    plane_update = call(plane_kernel, "plane_state", shape(tagged, BF16), [meta, chip, chip_other])
    serve(3, plane_update)
    spread(1, plane_update)
    table = after(block_table, plane_update)
    tables = [block_table] + [pool_shift(table, pool_count, r) for r in range(1, pool_count)]
    total = plane_update
    before = []
    reach = 1
    while reach < planes:
        received = to_later_planes(total, seq_count, reach)
        if len(inners) < 3:
            query = after(query_rows, total)
            inners.append(
                inner_part(1 + len(inners), 1, query, key_rows, value_rows, cumul)
            )
            first = (come[2], *shares[1], *tables) if reach == 1 else (*shares[3], *shares[2])
            received[0] = after(received[0], inners[-1], *first)
        final = 2 * reach >= planes
        prefix, *rest = call(
            functools.partial(scan_kernel, reach),
            "scan_state",
            [shape(tagged, BF16)] * (1 if final else 2),
            [meta, *received, *before, plane_update],
        )
        if reach == 1:
            serve(4, prefix)
            spread(2, prefix)
            spread(3, prefix)
        before, total = [prefix], (rest or [None])[0]
        reach *= 2
    prefix_other = to_other_row(prefix, seq_count, 1)
    residual_other = seq_xor(after(residual, prefix), seq_count, 1)
    serve(5, prefix)
    own_state, away_state = call(
        start_kernel,
        "start_state",
        [shape((heads, HD, HD), BF16)] * 2,
        [meta, update, update_other, chip_other, prefix, prefix_other],
    )
    other_state = seq_xor(away_state, seq_count, 1)
    spread(4, own_state)
    other_state = after(other_state, come[4])

    mixed = pl.pallas_call(
        mixed_kernel,
        name="mixed",
        grid=(INNER,),
        out_shape=[shape((rows_here, wide), BF16)] * pool_count,
        in_specs=[SMEM, by_share]
        + [VMEM] * 3
        + [pl.BlockSpec((1, share, rows), lambda g: (g, 0, 0))]
        + [pl.BlockSpec((share, HD, HD), lambda g: (g, 0, 0))] * 2,
        out_specs=[pl.BlockSpec((rows_here, share * HD), lambda g: (0, g))] * pool_count,
        scratch_shapes=[pltpu.VMEM((rows, share * HD), F32)],
        cost_estimate=LIGHT,
        compiler_params=params(12),
    )(meta, in_hbm(query_rows), *inners, cumul, own_state, other_state)
    mixed_other = [seq_xor(part, seq_count, 1) for part in mixed]
    both = []

    def project(g, *first):
        blocks = arrivals(g)
        count = len(blocks)
        out_wide = count * width
        joins = not both
        sources = [after(both[0], *first)] if both else [*mixed, *mixed_other]
        joined = [shape((pool_count, chip_rows, wide), BF16)] if joins else []
        mine, *away = call(
            functools.partial(project_kernel, pool_count if joins else 0, count),
            "project",
            [shape((chip_rows, out_wide), F32)]
            + [shape((chip_rows, out_wide), BF16)] * (pool_count - 1)
            + joined,
            [*sources, *blocks],
            mib=12,
        )
        if joins:
            both.append(away.pop())
        arrived = [pool_shift(away[r - 1], pool_count, r) for r in range(1, pool_count)]
        return mine, arrived

    def cache(g, projected, sums, *first):
        mine, arrived = projected
        kv = kv_of(g)
        count = len(starts[g])
        out_wide = count * width
        around = [residual, residual_other, norm_gain.reshape(1, -1)]
        if width % HD:
            around = [
                jnp.concatenate([lax.dynamic_slice_in_dim(a, s, width, 1) for s in starts[g]], 1)
                for a in around
            ]
        return call(
            functools.partial(
                cache_kernel,
                not sums,
                count,
                pool_count,
                len(kv),
                width,
                3 + sum(len(x) for x in starts[:g]),
            ),
            "cache",
            [shape((rows_here, cache_width), F32)] * 2 + [shape((rows_here, HD), F32)] * 2,
            [
                meta,
                after(mine, *first),
                *around,
                *kv,
                *arrived,
                *sums,
            ],
            [
                pltpu.VMEM((out_wide, cache_width), BF16),
                pltpu.VMEM((chip_rows, out_wide), BF16),
                pltpu.VMEM((chip_rows, out_wide), BF16),
                pltpu.SemaphoreType.DMA((2 * count,)),
            ],
            mib=12,
            far=() if width % HD else (2, 3),
        )

    projected = {0: project(0)}
    done = (projected[0][0],)
    sums = ()
    cached = 0

    def reduce_one():
        nonlocal sums, done, cached
        sums = cache(cached, projected[cached], sums, *done)
        done = (sums[2],)
        cached += 1

    for g in range(1, steps + 1):
        if g > 2:
            done = (*done, *[come[m] for m in (2 * g - 1, 2 * g) if m <= last])
        projected[g] = project(g, *done)
        done = (projected[g][0],)
        if g == 1:
            serve(6, *done)
            continue
        if g == 2:
            done = (*done, residual_other)
            reduce_one()
        for n in (2 * g + 3, 2 * g + 4):
            if n not in come and n <= last:
                serve(n, come[n - 2], *done)
                done = (*done, come[n - 2])
        while g < steps and cached <= g - 1:
            reduce_one()
    while cached <= steps:
        reduce_one()
    own_total, other_total, own_square, other_square = sums
    cache_rows = call(
        functools.partial(finish_kernel, width * seq_count),
        "finish",
        shape((rows_here, cache_width), BF16),
        [
            own_total,
            own_square,
            seq_xor(other_total, seq_count, 1),
            seq_xor(other_square, seq_count, 1),
        ],
    )
    pages = [cache_rows] + [pool_shift(cache_rows, pool_count, r) for r in range(1, pool_count)]
    page_cache = call(
        functools.partial(place_kernel, pool_count),
        "place",
        shape((slot_count, PAGE, cache_width), BF16),
        [meta, *tables, *pages],
    )
    return page_cache.reshape(1, 1, slot_count, PAGE, cache_width)


def solution(mesh):
    placed = (
        P("seq", "pool"),
        P("seq", "pool"),
        P("seq", "pool"),
        P("pool", "seq"),
        P(("seq", "pool"), None),
        P("pool", "seq"),
        P(),
        P("seq", None),
        P(("seq", "pool"), None),
    )
    return jax.shard_map(
        on_device,
        mesh=mesh,
        in_specs=placed,
        out_specs=P("seq", "pool", None, None, None),
        check_vma=False,
    )
```

```python
import functools

import jax
import jax.numpy as jnp
from jax import lax
from jax.experimental import pallas as pl
from jax.experimental.pallas import tpu as pltpu
from jax.sharding import PartitionSpec as P

HD = 128
PAGE = 128
INNER = 4
TAG = 16
EPS = 1e-05
BF16 = jnp.bfloat16
F32 = jnp.float32
SMEM = pl.BlockSpec(memory_space=pltpu.SMEM)
VMEM = pl.BlockSpec(memory_space=pltpu.VMEM)
FAR = pl.BlockSpec(memory_space=pltpu.HBM)
LIGHT = pl.CostEstimate(flops=1, bytes_accessed=1, transcendentals=0)


def params(mib):
    return pltpu.CompilerParams(vmem_limit_bytes=mib * 2**20)


def call(body, name, out_shape, args, scratch=(), mib=8, far=()):
    return pl.pallas_call(
        body,
        name=name,
        out_shape=out_shape,
        in_specs=[
            SMEM if a.dtype == jnp.int32 else FAR if n in far else VMEM
            for n, a in enumerate(args)
        ],
        out_specs=jax.tree.map(lambda _: VMEM, out_shape),
        scratch_shapes=list(scratch),
        cost_estimate=LIGHT,
        compiler_params=params(mib),
    )(*[in_hbm(a) if n in far else a for n, a in enumerate(args)])


def after(value, *first):
    return lax.optimization_barrier((value, *first))[0]


def in_hbm(value):
    return pltpu.with_memory_space_constraint(value, pltpu.HBM)


def shape(dims, dtype):
    return jax.ShapeDtypeStruct(dims, dtype)


def seq_xor(value, seq_count, bits):
    return lax.ppermute(value, "seq", [(j, j ^ bits) for j in range(seq_count)])


def seq_index(plane, row, core):
    return plane * INNER + row * 2 + core


def to_other_row(value, seq_count, first_plane):
    pairs = []
    for plane in range(first_plane, seq_count // INNER):
        for row in range(2):
            core = row if plane == 0 else 1 - row
            pairs.append((seq_index(plane, row, core), seq_index(plane, 1 - row, row)))
    return lax.ppermute(value, "seq", pairs)


def to_later_planes(value, seq_count, reach):
    planes = seq_count // INNER
    return [
        lax.ppermute(
            value,
            "seq",
            [
                (seq_index(plane, row, 1 - row), seq_index(plane + by, row, 1 - row))
                for plane in range(reach - 1, planes - by, 2 * reach)
                for row in range(2)
            ],
        )
        for by in range(1, reach + 1)
    ]


def pool_shift(value, pool_count, by):
    return lax.ppermute(value, "pool", [(i, (i + by) % pool_count) for i in range(pool_count)])


def ring_chip(spot, planes):
    if isinstance(spot, int):
        return spot * 2 if spot < planes else (2 * planes - 1 - spot) * 2 + 1
    return jnp.where(spot < planes, spot * 2, (2 * planes - 1 - spot) * 2 + 1)


def ring_step(value, seq_count):
    planes = seq_count // INNER
    length = 2 * planes
    pairs = []
    for spot in range(length):
        for core, by in ((0, 1), (1, -1)):
            source, target = ring_chip(spot, planes), ring_chip((spot + by) % length, planes)
            pairs.append((source * 2 + core, target * 2 + core))
    return lax.ppermute(value, "seq", pairs)


def columns(lines):
    repeat = -(-8 // lines.shape[0])
    return jnp.concatenate([lines] * repeat).T


def tag_of(total):
    term = lax.broadcasted_iota(jnp.int32, (TAG, HD), 0)
    high = total.astype(BF16).astype(F32)
    middle = (total - high).astype(BF16).astype(F32)
    low = total - high - middle
    terms = jnp.where(
        term == 0, high, jnp.where(term == 1, middle, jnp.where(term == 2, low, 0.0))
    )
    return terms.astype(BF16)


def update_kernel(key, value, decay, cumul, out):
    _, share, rows = cumul.shape
    step = pl.program_id(0)

    @pl.when(step == 0)
    def _():
        before = lax.broadcasted_iota(jnp.int32, (rows, rows), 0)
        upto = lax.broadcasted_iota(jnp.int32, (rows, rows), 1)
        ones = (before <= upto).astype(F32)
        total = jnp.dot(
            decay[...], ones, precision=lax.Precision.HIGHEST, preferred_element_type=F32
        )
        for n in range(INNER):
            cumul[n] = total[n * share : (n + 1) * share]

    lines = cumul[step]
    weights = columns(jnp.exp(lines[:, rows - 1 :] - lines))
    for i in range(share):
        lane = slice(i * HD, (i + 1) * HD)
        weighted = (key[:, lane].astype(F32) * weights[:, i : i + 1]).astype(BF16)
        update = lax.dot_general(
            weighted, value[:, lane], (((0,), (0,)), ((), ())), preferred_element_type=F32
        )
        out[i, :HD, :] = update.astype(BF16)
        out[i, HD:, :] = tag_of(lines[i : i + 1, rows - 1 :])


def state_of(ref, i):
    return ref[i, :HD, :].astype(F32)


def total_of(ref, i):
    return jnp.sum(ref[i, HD:, :].astype(F32), axis=0, keepdims=True)


def either(choice, one, two, i):
    state = jnp.where(choice, state_of(one, i), state_of(two, i))
    return state, jnp.where(choice, total_of(one, i), total_of(two, i))


def chip_kernel(meta, own, other, out):
    lead = meta[0] % 2 == 0
    for i in range(out.shape[0]):
        state, total = either(lead, own, other, i)
        after_state, after_total = either(lead, other, own, i)
        out[i, :HD, :] = (jnp.exp(after_total) * state + after_state).astype(BF16)
        out[i, HD:, :] = tag_of(total + after_total)


def plane_kernel(meta, own, other, out):
    row = meta[0] // 2
    for i in range(out.shape[0]):
        h = row * out.shape[0] + i
        state, total = either(row == 0, own, other, h)
        after_state, after_total = either(row == 0, other, own, h)
        out[i, :HD, :] = (jnp.exp(after_total) * state + after_state).astype(BF16)
        out[i, HD:, :] = tag_of(total + after_total)


def scan_kernel(reach, meta, *refs):
    received, refs = refs[:reach], refs[reach:]
    if reach > 1:
        before, *refs = refs
    own, *outs = refs
    upper = meta[1] // reach % 2 == 1
    by = meta[1] % reach
    for i in range(own.shape[0]):
        state, total = state_of(received[0], i), total_of(received[0], i)
        for n in range(1, reach):
            state = jnp.where(by == n, state_of(received[n], i), state)
            total = jnp.where(by == n, total_of(received[n], i), total)
        state = jnp.where(upper, state, 0.0)
        total = jnp.where(upper, total, 0.0)
        if reach > 1:
            later = total_of(before, i)
            state = jnp.exp(later) * state + state_of(before, i)
            total = total + later
        outs[0][i, :HD, :] = state.astype(BF16)
        outs[0][i, HD:, :] = tag_of(total)
        if len(outs) > 1:
            later = total_of(own, i)
            outs[1][i, :HD, :] = (jnp.exp(later) * state + state_of(own, i)).astype(BF16)
            outs[1][i, HD:, :] = tag_of(total + later)


def start_kernel(meta, own, other, row_update, prefix, other_prefix, mine, away):
    row, lead = meta[0] // 2, meta[0] % 2 == 0
    half = prefix.shape[0]
    for i in range(mine.shape[0]):
        here = row == i // half
        state = jnp.where(here, state_of(prefix, i % half), state_of(other_prefix, i % half))
        grown = jnp.exp(total_of(row_update, i)) * state + state_of(row_update, i)
        state = jnp.where(row == 0, state, grown)
        update, total = either(lead, own, other, i)
        later = jnp.exp(total) * state + update
        mine[i] = jnp.where(lead, state, later).astype(BF16)
        away[i] = jnp.where(lead, later, state).astype(BF16)


def inner_kernel(query, key, value, cumul, out):
    rows = query.shape[0]
    half = min(256, rows)
    lines = cumul[0]
    upright = columns(lines)
    row = lax.broadcasted_iota(jnp.int32, (half, half), 0)
    col = lax.broadcasted_iota(jnp.int32, (half, half), 1)
    bar = jnp.where(row >= col, 0.0, -1e30)
    for i in range(lines.shape[0]):
        lane = slice(i * HD, (i + 1) * HD)
        for at in range(0, rows, half):
            here = slice(at, at + half)
            total = None
            for start in range(0, at + half, half):
                there = slice(start, start + half)
                products = lax.dot_general(
                    query[here, lane],
                    key[there, lane],
                    (((1,), (1,)), ((), ())),
                    preferred_element_type=F32,
                )
                gap = upright[here, i : i + 1] - lines[i : i + 1, there]
                if start == at:
                    gap = gap + bar
                scores = (products * jnp.exp(gap)).astype(BF16)
                part = jnp.dot(scores, value[there, lane], preferred_element_type=F32)
                total = part if total is None else total + part
            out[here, lane] = total


def mixed_kernel(meta, query, *refs):
    inners = refs[:3]
    cumul, *refs = refs[3:]
    own_state, other_state, *outs, held = refs
    pool_count, rows = len(outs), outs[0].shape[0]
    step = pl.program_id(0)
    gathers = meta[0] // 2 + meta[0] % 2 == 1
    me = meta[2]
    lines = cumul[0]
    grown = columns(jnp.exp(lines))
    for i in range(lines.shape[0]):
        lane = slice(i * HD, (i + 1) * HD)
        state = jnp.where(gathers, own_state[i], other_state[i])
        outer = jnp.dot(query[:, lane], state, preferred_element_type=F32)
        held[:, lane] = outer * grown[:, i : i + 1]
    for n in range(INNER):

        @pl.when(step == n)
        def _():
            part = (n if n < 2 else 0) * held.shape[1]
            held[...] = held[...] + inners[max(0, n - 1)][:, part : part + held.shape[1]]

    for r in range(pool_count):
        start = pl.multiple_of(lax.rem(me + r, pool_count) * rows, rows)
        for i in range(lines.shape[0]):
            lane = slice(i * HD, (i + 1) * HD)
            retained = held[pl.ds(start, rows), lane]
            mean = jnp.mean(retained * retained, axis=-1, keepdims=True)
            outs[r][:, lane] = (retained * lax.rsqrt(mean + EPS)).astype(BF16)


def pack_kernel(weight, kv, out):
    depth, width = weight.shape
    rows = kv.shape[0]
    out[:depth, :] = weight[...]
    for c in range(kv.shape[1] // width):
        here = slice(c * width, (c + 1) * width)
        out[depth + c * rows : depth + (c + 1) * rows, :] = kv[:, here]


def cut_kernel(block, out):
    out[...] = block[block.shape[0] - out.shape[0] :, :]


def widen_kernel(meta, block, *refs):
    *shares, out = refs
    rows = shares[0].shape[0]
    depth = block.shape[0] - rows
    out[:depth, :] = block[:depth, :]
    for r, part in enumerate(shares):
        share = lax.rem(meta[2] + len(shares) - r, len(shares))
        start = pl.multiple_of(depth + share * rows, rows)
        out[pl.ds(start, rows), :] = part[...]


def project_kernel(joins, parts, *refs):
    if joins:
        both = refs[-1]
        rows = refs[0].shape[0]
        for r in range(joins):
            both[r, :rows, :] = refs[r][...]
            both[r, rows:, :] = refs[joins + r][...]
        refs = refs[2 * joins : -1]
    else:
        both = refs[0]
        refs = refs[1:]
    blocks = refs[:parts]
    mine, *away = refs[parts:]
    pool_count, _, depth = both.shape
    width = blocks[0].shape[1]
    for r in list(range(1, pool_count)) + [0]:
        for p in range(parts):
            here = slice(p * width, (p + 1) * width)
            total = jnp.dot(both[r], blocks[p][:depth, :], preferred_element_type=F32)
            if r == 0:
                mine[:, here] = total
            else:
                away[r - 1][:, here] = total.astype(BF16)


def cache_kernel(first, parts, shares, kv_count, width, at, meta, mine, *refs):
    own_rows, other_rows, gain, *refs = refs
    kv, refs = refs[:kv_count], refs[kv_count:]
    *arrived, held, scaled, near, sems = refs
    arrived, sums = arrived[:-4], arrived[-4:]
    if not first:
        arrived, old = arrived[:-4], arrived[-4:]
    rows = own_rows.shape[0]
    whole = own_rows.shape[1] == parts * width
    copies = []
    for p in range(parts if not whole else 0):
        here = slice(p * width, (p + 1) * width)
        there = pl.ds(pl.multiple_of(meta[at + p], width), width)
        for n, source in enumerate((own_rows, other_rows)):
            target = near.at[n * rows : (n + 1) * rows, here]
            copies.append(
                pltpu.make_async_copy(source.at[:, there], target, sems.at[2 * p + n])
            )
            copies[-1].start()
    depth = width // shares
    chunks = held.shape[1] // width
    if kv_count == 1 and parts == 1 and kv[0].shape == held.shape:
        held[...] = kv[0][...]
    else:
        each = kv_count // parts
        for p in range(parts):
            for r in range(shares):
                source = kv[p * each + (r if each > 1 else 0)]
                share = lax.rem(meta[2] + shares - r, shares) if each > 1 else r
                start = p * width + share * depth
                if each > 1:
                    start = pl.multiple_of(start, depth)
                base = source.shape[0] - chunks * depth * (1 if each > 1 else shares - r)
                for c in range(chunks):
                    held[pl.ds(start, depth), c * width : (c + 1) * width] = source[
                        base + c * depth : base + (c + 1) * depth, :
                    ]
    for copy in copies:
        copy.wait()
    if whole:
        near[:rows, :] = own_rows[...]
        near[rows:, :] = other_rows[...]
    squares = 0.0
    for p in range(parts):
        here = slice(p * width, (p + 1) * width)
        there = here if whole else pl.ds(pl.multiple_of(meta[at + p], width), width)
        values = near[:, here].astype(F32) + mine[:, here]
        for part in arrived:
            values = values + part[:, here].astype(F32)
        squares = squares + jnp.sum(values * values, axis=-1, keepdims=True)
        scaled[:, here] = (values * gain[:, there]).astype(BF16)
    for n in range(2):
        here = slice(n * rows, (n + 1) * rows)
        product = jnp.dot(scaled[here, :], held[...], preferred_element_type=F32)
        if first:
            sums[n][...] = product
            sums[2 + n][...] = jnp.broadcast_to(squares[here], (rows, HD))
        else:
            sums[n][...] = old[n][...] + product
            sums[2 + n][...] = old[2 + n][...] + squares[here]


def finish_kernel(features, total, square, total_in, square_in, out):
    mean = (square[:, :1] + square_in[:, :1]) / features
    out[...] = ((total[...] + total_in[...]) * lax.rsqrt(mean + EPS)).astype(BF16)


def place_kernel(pool_count, meta, *refs):
    tables = refs[:pool_count]
    *pages, out = refs[pool_count:]
    me = meta[2]
    out[...] = jnp.zeros(out.shape, out.dtype)
    for table, part in zip(tables, pages):
        for p in range(part.shape[0] // PAGE):
            owner, slot = table[p, 0], table[p, 1]

            @pl.when(owner == me)
            def _():
                out[slot] = part[p * PAGE : (p + 1) * PAGE, :]


def inner_part(n, count, query_rows, key_rows, value_rows, cumul):
    rows = query_rows.shape[0]
    _, share, _ = cumul.shape
    there = pl.BlockSpec((rows, share * HD), lambda i: (0, i + n))
    return pl.pallas_call(
        inner_kernel,
        name="inner",
        grid=(count,),
        out_shape=shape((rows, count * share * HD), F32),
        in_specs=[there] * 3 + [pl.BlockSpec((1, share, rows), lambda i: (i + n, 0, 0))],
        out_specs=pl.BlockSpec((rows, share * HD), lambda i: (0, i)),
        cost_estimate=LIGHT,
        compiler_params=params(12),
    )(in_hbm(query_rows), in_hbm(key_rows), in_hbm(value_rows), cumul)


def on_device(
    query_rows,
    key_rows,
    value_rows,
    log_decay,
    residual,
    out_weight,
    norm_gain,
    kv_weight,
    block_table,
):
    seq_count = lax.axis_size("seq")
    pool_count = lax.axis_size("pool")
    planes = seq_count // INNER
    length = 2 * planes
    index = lax.axis_index("seq")
    me = lax.axis_index("pool")
    place = index % INNER
    plane = index // INNER
    core = index % 2
    spot = jnp.where(place < 2, plane, length - 1 - plane)
    width = out_weight.shape[1]
    steps = length // 2
    starts = []
    for g in range(steps + 1):
        chip = ring_chip((spot + length + jnp.where(core == 0, -g, g)) % length, planes)
        cores = [core] if g in (0, steps) else [core, 1 - core]
        starts.append([(chip * 2 + c) * width for c in cores])
    meta = jnp.stack([place, plane, me] + sum(starts, [])).astype(jnp.int32)
    rows, wide = query_rows.shape
    heads = wide // HD
    share = heads // INNER
    rows_here = residual.shape[0]
    cache_width = kv_weight.shape[1]
    pages_here = block_table.shape[0]
    slot_count = 2 * pages_here
    chip_rows = 2 * rows_here

    kv_share = kv_weight.shape[0] // pool_count
    kv_rows = kv_share * cache_width // width
    kv_own = lax.dynamic_slice_in_dim(kv_weight, me * kv_share, kv_share, 0)
    packed = shape((out_weight.shape[0] + kv_rows, width), BF16)
    weights = call(pack_kernel, "pack", packed, [out_weight, kv_own])
    last = 2 * steps - 1
    come = {-1: weights, 0: seq_xor(weights, seq_count, 1)}
    shares = {}

    def spread(n, *first):
        part = call(
            cut_kernel,
            "cut",
            shape((kv_rows, width), BF16),
            [after(come[n], *first) if first else come[n]],
        )
        shares[n] = [part] + [pool_shift(part, pool_count, r) for r in range(1, pool_count)]
        return shares[n]

    def serve(n, *first):
        block = after(come[n - 2], *first) if first else come[n - 2]
        if n - 2 in (3, 4):
            whole = shape((out_weight.shape[0] + kv_rows * pool_count, width), BF16)
            block = call(widen_kernel, "widen", whole, [meta, block, *shares[n - 2]])
        come[n] = ring_step(block, seq_count)
        return come[n]

    def arrivals(g):
        if g == 0:
            return [come[-1]]
        if g == steps:
            return [come[last]]
        return [come[2 * g - 1], come[2 * g]]

    def kv_of(g):
        if g == 0:
            return [kv_weight]
        if g < 3:
            return [part for n in (2 * g - 1, 2 * g) for part in shares[n]]
        return arrivals(g)

    serve(1)

    by_share = pl.BlockSpec((rows, share * HD), lambda g: (0, g))
    cumul, update = pl.pallas_call(
        update_kernel,
        name="update",
        grid=(INNER,),
        out_shape=[shape((INNER, share, rows), F32), shape((heads, HD + TAG, HD), BF16)],
        in_specs=[by_share, by_share, pl.BlockSpec((heads, rows), lambda g: (0, 0))],
        out_specs=[
            pl.BlockSpec((INNER, share, rows), lambda g: (0, 0, 0)),
            pl.BlockSpec((share, HD + TAG, HD), lambda g: (g, 0, 0)),
        ],
        cost_estimate=LIGHT,
        compiler_params=params(12),
    )(in_hbm(key_rows), in_hbm(value_rows), log_decay)
    update = after(update, come[0])
    update_other = seq_xor(update, seq_count, 1)
    serve(2, update_other)
    chip = call(
        chip_kernel, "chip_state", shape(update.shape, BF16), [meta, update, update_other]
    )
    chip_other = to_other_row(chip, seq_count, 0)
    inners = [inner_part(0, INNER // 2, query_rows, key_rows, value_rows, cumul)]
    chip_other = after(chip_other, inners[0], come[1])
    tagged = (heads // 2, HD + TAG, HD)
    plane_update = call(plane_kernel, "plane_state", shape(tagged, BF16), [meta, chip, chip_other])
    serve(3, plane_update)
    spread(1, plane_update)
    table = after(block_table, plane_update)
    tables = [block_table] + [pool_shift(table, pool_count, r) for r in range(1, pool_count)]
    total = plane_update
    before = []
    reach = 1
    while reach < planes:
        received = to_later_planes(total, seq_count, reach)
        if len(inners) < 3:
            query = after(query_rows, total)
            inners.append(
                inner_part(1 + len(inners), 1, query, key_rows, value_rows, cumul)
            )
            first = (come[2], *shares[1], *tables) if reach == 1 else (*shares[3], *shares[2])
            received[0] = after(received[0], inners[-1], *first)
        final = 2 * reach >= planes
        prefix, *rest = call(
            functools.partial(scan_kernel, reach),
            "scan_state",
            [shape(tagged, BF16)] * (1 if final else 2),
            [meta, *received, *before, plane_update],
        )
        if reach == 1:
            serve(4, prefix)
            spread(2, prefix)
            spread(3, prefix)
        before, total = [prefix], (rest or [None])[0]
        reach *= 2
    prefix_other = to_other_row(prefix, seq_count, 1)
    residual_other = seq_xor(after(residual, prefix), seq_count, 1)
    serve(5, prefix)
    own_state, away_state = call(
        start_kernel,
        "start_state",
        [shape((heads, HD, HD), BF16)] * 2,
        [meta, update, update_other, chip_other, prefix, prefix_other],
    )
    other_state = seq_xor(away_state, seq_count, 1)
    spread(4, own_state)
    other_state = after(other_state, come[4])

    mixed = pl.pallas_call(
        mixed_kernel,
        name="mixed",
        grid=(INNER,),
        out_shape=[shape((rows_here, wide), BF16)] * pool_count,
        in_specs=[SMEM, by_share]
        + [VMEM] * 3
        + [pl.BlockSpec((1, share, rows), lambda g: (g, 0, 0))]
        + [pl.BlockSpec((share, HD, HD), lambda g: (g, 0, 0))] * 2,
        out_specs=[pl.BlockSpec((rows_here, share * HD), lambda g: (0, g))] * pool_count,
        scratch_shapes=[pltpu.VMEM((rows, share * HD), F32)],
        cost_estimate=LIGHT,
        compiler_params=params(12),
    )(meta, in_hbm(query_rows), *inners, cumul, own_state, other_state)
    mixed_other = [seq_xor(part, seq_count, 1) for part in mixed]
    both = []

    def project(g, *first):
        blocks = arrivals(g)
        count = len(blocks)
        out_wide = count * width
        joins = not both
        sources = [after(both[0], *first)] if both else [*mixed, *mixed_other]
        joined = [shape((pool_count, chip_rows, wide), BF16)] if joins else []
        mine, *away = call(
            functools.partial(project_kernel, pool_count if joins else 0, count),
            "project",
            [shape((chip_rows, out_wide), F32)]
            + [shape((chip_rows, out_wide), BF16)] * (pool_count - 1)
            + joined,
            [*sources, *blocks],
            mib=12,
        )
        if joins:
            both.append(away.pop())
        arrived = [pool_shift(away[r - 1], pool_count, r) for r in range(1, pool_count)]
        return mine, arrived

    def cache(g, projected, sums, *first):
        mine, arrived = projected
        kv = kv_of(g)
        count = len(starts[g])
        out_wide = count * width
        around = [residual, residual_other, norm_gain.reshape(1, -1)]
        if width % HD:
            around = [
                jnp.concatenate([lax.dynamic_slice_in_dim(a, s, width, 1) for s in starts[g]], 1)
                for a in around
            ]
        return call(
            functools.partial(
                cache_kernel,
                not sums,
                count,
                pool_count,
                len(kv),
                width,
                3 + sum(len(x) for x in starts[:g]),
            ),
            "cache",
            [shape((rows_here, cache_width), F32)] * 2 + [shape((rows_here, HD), F32)] * 2,
            [
                meta,
                after(mine, *first),
                *around,
                *kv,
                *arrived,
                *sums,
            ],
            [
                pltpu.VMEM((out_wide, cache_width), BF16),
                pltpu.VMEM((chip_rows, out_wide), BF16),
                pltpu.VMEM((chip_rows, out_wide), BF16),
                pltpu.SemaphoreType.DMA((2 * count,)),
            ],
            mib=12,
            far=() if width % HD else (2, 3),
        )

    projected = {0: project(0)}
    done = (projected[0][0],)
    sums = ()
    cached = 0

    def reduce_one():
        nonlocal sums, done, cached
        sums = cache(cached, projected[cached], sums, *done)
        done = (sums[2],)
        cached += 1

    for g in range(1, steps + 1):
        if g > 2:
            done = (*done, *[come[m] for m in (2 * g - 1, 2 * g) if m <= last])
        projected[g] = project(g, *done)
        done = (projected[g][0],)
        if g == 1:
            serve(6)
            continue
        if g == 2:
            done = (*done, residual_other)
            reduce_one()
            reduce_one()
        for n in (2 * g + 3, 2 * g + 4):
            if n not in come and n <= last:
                serve(n)
        while g < steps and cached <= g - 1:
            reduce_one()
    while cached <= steps:
        reduce_one()
    own_total, other_total, own_square, other_square = sums
    cache_rows = call(
        functools.partial(finish_kernel, width * seq_count),
        "finish",
        shape((rows_here, cache_width), BF16),
        [
            own_total,
            own_square,
            seq_xor(other_total, seq_count, 1),
            seq_xor(other_square, seq_count, 1),
        ],
    )
    pages = [cache_rows] + [pool_shift(cache_rows, pool_count, r) for r in range(1, pool_count)]
    page_cache = call(
        functools.partial(place_kernel, pool_count),
        "place",
        shape((slot_count, PAGE, cache_width), BF16),
        [meta, *tables, *pages],
    )
    return page_cache.reshape(1, 1, slot_count, PAGE, cache_width)


def solution(mesh):
    placed = (
        P("seq", "pool"),
        P("seq", "pool"),
        P("seq", "pool"),
        P("pool", "seq"),
        P(("seq", "pool"), None),
        P("pool", "seq"),
        P(),
        P("seq", None),
        P(("seq", "pool"), None),
    )
    return jax.shard_map(
        on_device,
        mesh=mesh,
        in_specs=placed,
        out_specs=P("seq", "pool", None, None, None),
        check_vma=False,
    )
```

```python
import functools

import jax
import jax.numpy as jnp
from jax import lax
from jax.experimental import pallas as pl
from jax.experimental.pallas import tpu as pltpu
from jax.sharding import PartitionSpec as P

HD = 128
PAGE = 128
INNER = 4
TAG = 16
EPS = 1e-05
BF16 = jnp.bfloat16
F32 = jnp.float32
SMEM = pl.BlockSpec(memory_space=pltpu.SMEM)
VMEM = pl.BlockSpec(memory_space=pltpu.VMEM)
FAR = pl.BlockSpec(memory_space=pltpu.HBM)
LIGHT = pl.CostEstimate(flops=1, bytes_accessed=1, transcendentals=0)


def params(mib):
    return pltpu.CompilerParams(vmem_limit_bytes=mib * 2**20)


def call(body, name, out_shape, args, scratch=(), mib=8, far=()):
    return pl.pallas_call(
        body,
        name=name,
        out_shape=out_shape,
        in_specs=[
            SMEM if a.dtype == jnp.int32 else FAR if n in far else VMEM
            for n, a in enumerate(args)
        ],
        out_specs=jax.tree.map(lambda _: VMEM, out_shape),
        scratch_shapes=list(scratch),
        cost_estimate=LIGHT,
        compiler_params=params(mib),
    )(*[in_hbm(a) if n in far else a for n, a in enumerate(args)])


def after(value, *first):
    return lax.optimization_barrier((value, *first))[0]


def in_hbm(value):
    return pltpu.with_memory_space_constraint(value, pltpu.HBM)


def shape(dims, dtype):
    return jax.ShapeDtypeStruct(dims, dtype)


def seq_xor(value, seq_count, bits):
    return lax.ppermute(value, "seq", [(j, j ^ bits) for j in range(seq_count)])


def seq_index(plane, row, core):
    return plane * INNER + row * 2 + core


def to_other_row(value, seq_count, first_plane):
    pairs = []
    for plane in range(first_plane, seq_count // INNER):
        for row in range(2):
            core = row if plane == 0 else 1 - row
            pairs.append((seq_index(plane, row, core), seq_index(plane, 1 - row, row)))
    return lax.ppermute(value, "seq", pairs)


def to_later_planes(value, seq_count, reach):
    planes = seq_count // INNER
    return [
        lax.ppermute(
            value,
            "seq",
            [
                (seq_index(plane, row, 1 - row), seq_index(plane + by, row, 1 - row))
                for plane in range(reach - 1, planes - by, 2 * reach)
                for row in range(2)
            ],
        )
        for by in range(1, reach + 1)
    ]


def pool_shift(value, pool_count, by):
    return lax.ppermute(value, "pool", [(i, (i + by) % pool_count) for i in range(pool_count)])


def ring_chip(spot, planes):
    if isinstance(spot, int):
        return spot * 2 if spot < planes else (2 * planes - 1 - spot) * 2 + 1
    return jnp.where(spot < planes, spot * 2, (2 * planes - 1 - spot) * 2 + 1)


def ring_step(value, seq_count):
    planes = seq_count // INNER
    length = 2 * planes
    pairs = []
    for spot in range(length):
        for core, by in ((0, 1), (1, -1)):
            source, target = ring_chip(spot, planes), ring_chip((spot + by) % length, planes)
            pairs.append((source * 2 + core, target * 2 + core))
    return lax.ppermute(value, "seq", pairs)


def columns(lines):
    repeat = -(-8 // lines.shape[0])
    return jnp.concatenate([lines] * repeat).T


def tag_of(total):
    term = lax.broadcasted_iota(jnp.int32, (TAG, HD), 0)
    high = total.astype(BF16).astype(F32)
    middle = (total - high).astype(BF16).astype(F32)
    low = total - high - middle
    terms = jnp.where(
        term == 0, high, jnp.where(term == 1, middle, jnp.where(term == 2, low, 0.0))
    )
    return terms.astype(BF16)


def update_kernel(key, value, decay, cumul, out):
    _, share, rows = cumul.shape
    step = pl.program_id(0)

    @pl.when(step == 0)
    def _():
        before = lax.broadcasted_iota(jnp.int32, (rows, rows), 0)
        upto = lax.broadcasted_iota(jnp.int32, (rows, rows), 1)
        ones = (before <= upto).astype(F32)
        total = jnp.dot(
            decay[...], ones, precision=lax.Precision.HIGHEST, preferred_element_type=F32
        )
        for n in range(INNER):
            cumul[n] = total[n * share : (n + 1) * share]

    lines = cumul[step]
    weights = columns(jnp.exp(lines[:, rows - 1 :] - lines))
    for i in range(share):
        lane = slice(i * HD, (i + 1) * HD)
        weighted = (key[:, lane].astype(F32) * weights[:, i : i + 1]).astype(BF16)
        update = lax.dot_general(
            weighted, value[:, lane], (((0,), (0,)), ((), ())), preferred_element_type=F32
        )
        out[i, :HD, :] = update.astype(BF16)
        out[i, HD:, :] = tag_of(lines[i : i + 1, rows - 1 :])


def state_of(ref, i):
    return ref[i, :HD, :].astype(F32)


def total_of(ref, i):
    return jnp.sum(ref[i, HD:, :].astype(F32), axis=0, keepdims=True)


def either(choice, one, two, i):
    state = jnp.where(choice, state_of(one, i), state_of(two, i))
    return state, jnp.where(choice, total_of(one, i), total_of(two, i))


def chip_kernel(meta, own, other, out):
    lead = meta[0] % 2 == 0
    for i in range(out.shape[0]):
        state, total = either(lead, own, other, i)
        after_state, after_total = either(lead, other, own, i)
        out[i, :HD, :] = (jnp.exp(after_total) * state + after_state).astype(BF16)
        out[i, HD:, :] = tag_of(total + after_total)


def plane_kernel(meta, own, other, out):
    row = meta[0] // 2
    for i in range(out.shape[0]):
        h = row * out.shape[0] + i
        state, total = either(row == 0, own, other, h)
        after_state, after_total = either(row == 0, other, own, h)
        out[i, :HD, :] = (jnp.exp(after_total) * state + after_state).astype(BF16)
        out[i, HD:, :] = tag_of(total + after_total)


def scan_kernel(reach, meta, *refs):
    received, refs = refs[:reach], refs[reach:]
    if reach > 1:
        before, *refs = refs
    own, *outs = refs
    upper = meta[1] // reach % 2 == 1
    by = meta[1] % reach
    for i in range(own.shape[0]):
        state, total = state_of(received[0], i), total_of(received[0], i)
        for n in range(1, reach):
            state = jnp.where(by == n, state_of(received[n], i), state)
            total = jnp.where(by == n, total_of(received[n], i), total)
        state = jnp.where(upper, state, 0.0)
        total = jnp.where(upper, total, 0.0)
        if reach > 1:
            later = total_of(before, i)
            state = jnp.exp(later) * state + state_of(before, i)
            total = total + later
        outs[0][i, :HD, :] = state.astype(BF16)
        outs[0][i, HD:, :] = tag_of(total)
        if len(outs) > 1:
            later = total_of(own, i)
            outs[1][i, :HD, :] = (jnp.exp(later) * state + state_of(own, i)).astype(BF16)
            outs[1][i, HD:, :] = tag_of(total + later)


def start_kernel(meta, own, other, row_update, prefix, other_prefix, mine, away):
    row, lead = meta[0] // 2, meta[0] % 2 == 0
    half = prefix.shape[0]
    for i in range(mine.shape[0]):
        here = row == i // half
        state = jnp.where(here, state_of(prefix, i % half), state_of(other_prefix, i % half))
        grown = jnp.exp(total_of(row_update, i)) * state + state_of(row_update, i)
        state = jnp.where(row == 0, state, grown)
        update, total = either(lead, own, other, i)
        later = jnp.exp(total) * state + update
        mine[i] = jnp.where(lead, state, later).astype(BF16)
        away[i] = jnp.where(lead, later, state).astype(BF16)


def inner_kernel(query, key, value, cumul, out):
    rows = query.shape[0]
    half = min(256, rows)
    lines = cumul[0]
    upright = columns(lines)
    row = lax.broadcasted_iota(jnp.int32, (half, half), 0)
    col = lax.broadcasted_iota(jnp.int32, (half, half), 1)
    bar = jnp.where(row >= col, 0.0, -1e30)
    for i in range(lines.shape[0]):
        lane = slice(i * HD, (i + 1) * HD)
        for at in range(0, rows, half):
            here = slice(at, at + half)
            total = None
            for start in range(0, at + half, half):
                there = slice(start, start + half)
                products = lax.dot_general(
                    query[here, lane],
                    key[there, lane],
                    (((1,), (1,)), ((), ())),
                    preferred_element_type=F32,
                )
                gap = upright[here, i : i + 1] - lines[i : i + 1, there]
                if start == at:
                    gap = gap + bar
                scores = (products * jnp.exp(gap)).astype(BF16)
                part = jnp.dot(scores, value[there, lane], preferred_element_type=F32)
                total = part if total is None else total + part
            out[here, lane] = total


def mixed_kernel(meta, query, *refs):
    inners = refs[:3]
    cumul, *refs = refs[3:]
    own_state, other_state, *outs, held = refs
    pool_count, rows = len(outs), outs[0].shape[0]
    step = pl.program_id(0)
    gathers = meta[0] // 2 + meta[0] % 2 == 1
    me = meta[2]
    lines = cumul[0]
    grown = columns(jnp.exp(lines))
    for i in range(lines.shape[0]):
        lane = slice(i * HD, (i + 1) * HD)
        state = jnp.where(gathers, own_state[i], other_state[i])
        outer = jnp.dot(query[:, lane], state, preferred_element_type=F32)
        held[:, lane] = outer * grown[:, i : i + 1]
    for n in range(INNER):

        @pl.when(step == n)
        def _():
            part = (n if n < 2 else 0) * held.shape[1]
            held[...] = held[...] + inners[max(0, n - 1)][:, part : part + held.shape[1]]

    for r in range(pool_count):
        start = pl.multiple_of(lax.rem(me + r, pool_count) * rows, rows)
        for i in range(lines.shape[0]):
            lane = slice(i * HD, (i + 1) * HD)
            retained = held[pl.ds(start, rows), lane]
            mean = jnp.mean(retained * retained, axis=-1, keepdims=True)
            outs[r][:, lane] = (retained * lax.rsqrt(mean + EPS)).astype(BF16)


def pack_kernel(weight, kv, out):
    depth, width = weight.shape
    rows = kv.shape[0]
    out[:depth, :] = weight[...]
    for c in range(kv.shape[1] // width):
        here = slice(c * width, (c + 1) * width)
        out[depth + c * rows : depth + (c + 1) * rows, :] = kv[:, here]


def cut_kernel(block, out):
    out[...] = block[block.shape[0] - out.shape[0] :, :]


def widen_kernel(meta, block, *refs):
    *shares, out = refs
    rows = shares[0].shape[0]
    depth = block.shape[0] - rows
    out[:depth, :] = block[:depth, :]
    for r, part in enumerate(shares):
        share = lax.rem(meta[2] + len(shares) - r, len(shares))
        start = pl.multiple_of(depth + share * rows, rows)
        out[pl.ds(start, rows), :] = part[...]


def project_kernel(joins, parts, *refs):
    if joins:
        both = refs[-1]
        rows = refs[0].shape[0]
        for r in range(joins):
            both[r, :rows, :] = refs[r][...]
            both[r, rows:, :] = refs[joins + r][...]
        refs = refs[2 * joins : -1]
    else:
        both = refs[0]
        refs = refs[1:]
    blocks = refs[:parts]
    mine, *away = refs[parts:]
    pool_count, _, depth = both.shape
    width = blocks[0].shape[1]
    for r in list(range(1, pool_count)) + [0]:
        for p in range(parts):
            here = slice(p * width, (p + 1) * width)
            total = jnp.dot(both[r], blocks[p][:depth, :], preferred_element_type=F32)
            if r == 0:
                mine[:, here] = total
            else:
                away[r - 1][:, here] = total.astype(BF16)


def cache_kernel(first, parts, shares, kv_count, width, at, meta, mine, *refs):
    own_rows, other_rows, gain, *refs = refs
    kv, refs = refs[:kv_count], refs[kv_count:]
    *arrived, held, scaled, near, sems = refs
    arrived, sums = arrived[:-4], arrived[-4:]
    if not first:
        arrived, old = arrived[:-4], arrived[-4:]
    rows = own_rows.shape[0]
    whole = own_rows.shape[1] == parts * width
    copies = []
    for p in range(parts if not whole else 0):
        here = slice(p * width, (p + 1) * width)
        there = pl.ds(pl.multiple_of(meta[at + p], width), width)
        for n, source in enumerate((own_rows, other_rows)):
            target = near.at[n * rows : (n + 1) * rows, here]
            copies.append(
                pltpu.make_async_copy(source.at[:, there], target, sems.at[2 * p + n])
            )
            copies[-1].start()
    depth = width // shares
    chunks = held.shape[1] // width
    if kv_count == 1 and parts == 1 and kv[0].shape == held.shape:
        held[...] = kv[0][...]
    else:
        each = kv_count // parts
        for p in range(parts):
            for r in range(shares):
                source = kv[p * each + (r if each > 1 else 0)]
                share = lax.rem(meta[2] + shares - r, shares) if each > 1 else r
                start = p * width + share * depth
                if each > 1:
                    start = pl.multiple_of(start, depth)
                base = source.shape[0] - chunks * depth * (1 if each > 1 else shares - r)
                for c in range(chunks):
                    held[pl.ds(start, depth), c * width : (c + 1) * width] = source[
                        base + c * depth : base + (c + 1) * depth, :
                    ]
    for copy in copies:
        copy.wait()
    if whole:
        near[:rows, :] = own_rows[...]
        near[rows:, :] = other_rows[...]
    squares = 0.0
    for p in range(parts):
        here = slice(p * width, (p + 1) * width)
        there = here if whole else pl.ds(pl.multiple_of(meta[at + p], width), width)
        values = near[:, here].astype(F32) + mine[:, here]
        for part in arrived:
            values = values + part[:, here].astype(F32)
        squares = squares + jnp.sum(values * values, axis=-1, keepdims=True)
        scaled[:, here] = (values * gain[:, there]).astype(BF16)
    for n in range(2):
        here = slice(n * rows, (n + 1) * rows)
        product = jnp.dot(scaled[here, :], held[...], preferred_element_type=F32)
        if first:
            sums[n][...] = product.astype(sums[n].dtype)
            sums[2 + n][...] = jnp.broadcast_to(squares[here], (rows, HD))
        else:
            sums[n][...] = (old[n][...] + product).astype(sums[n].dtype)
            sums[2 + n][...] = old[2 + n][...] + squares[here]


def finish_kernel(features, total, square, total_in, square_in, out):
    mean = (square[:, :1] + square_in[:, :1]) / features
    out[...] = ((total[...] + total_in[...].astype(F32)) * lax.rsqrt(mean + EPS)).astype(BF16)


def place_kernel(pool_count, meta, *refs):
    tables = refs[:pool_count]
    *pages, out = refs[pool_count:]
    me = meta[2]
    out[...] = jnp.zeros(out.shape, out.dtype)
    for table, part in zip(tables, pages):
        for p in range(part.shape[0] // PAGE):
            owner, slot = table[p, 0], table[p, 1]

            @pl.when(owner == me)
            def _():
                out[slot] = part[p * PAGE : (p + 1) * PAGE, :]


def inner_part(n, count, query_rows, key_rows, value_rows, cumul):
    rows = query_rows.shape[0]
    _, share, _ = cumul.shape
    there = pl.BlockSpec((rows, share * HD), lambda i: (0, i + n))
    return pl.pallas_call(
        inner_kernel,
        name="inner",
        grid=(count,),
        out_shape=shape((rows, count * share * HD), F32),
        in_specs=[there] * 3 + [pl.BlockSpec((1, share, rows), lambda i: (i + n, 0, 0))],
        out_specs=pl.BlockSpec((rows, share * HD), lambda i: (0, i)),
        cost_estimate=LIGHT,
        compiler_params=params(12),
    )(in_hbm(query_rows), in_hbm(key_rows), in_hbm(value_rows), cumul)


def on_device(
    query_rows,
    key_rows,
    value_rows,
    log_decay,
    residual,
    out_weight,
    norm_gain,
    kv_weight,
    block_table,
):
    seq_count = lax.axis_size("seq")
    pool_count = lax.axis_size("pool")
    planes = seq_count // INNER
    length = 2 * planes
    index = lax.axis_index("seq")
    me = lax.axis_index("pool")
    place = index % INNER
    plane = index // INNER
    core = index % 2
    spot = jnp.where(place < 2, plane, length - 1 - plane)
    width = out_weight.shape[1]
    steps = length // 2
    starts = []
    for g in range(steps + 1):
        chip = ring_chip((spot + length + jnp.where(core == 0, -g, g)) % length, planes)
        cores = [core] if g in (0, steps) else [core, 1 - core]
        starts.append([(chip * 2 + c) * width for c in cores])
    meta = jnp.stack([place, plane, me] + sum(starts, [])).astype(jnp.int32)
    rows, wide = query_rows.shape
    heads = wide // HD
    share = heads // INNER
    rows_here = residual.shape[0]
    cache_width = kv_weight.shape[1]
    pages_here = block_table.shape[0]
    slot_count = 2 * pages_here
    chip_rows = 2 * rows_here

    kv_share = kv_weight.shape[0] // pool_count
    kv_rows = kv_share * cache_width // width
    kv_own = lax.dynamic_slice_in_dim(kv_weight, me * kv_share, kv_share, 0)
    packed = shape((out_weight.shape[0] + kv_rows, width), BF16)
    weights = call(pack_kernel, "pack", packed, [out_weight, kv_own])
    last = 2 * steps - 1
    come = {-1: weights, 0: seq_xor(weights, seq_count, 1)}
    shares = {}

    def spread(n, *first):
        part = call(
            cut_kernel,
            "cut",
            shape((kv_rows, width), BF16),
            [after(come[n], *first) if first else come[n]],
        )
        shares[n] = [part] + [pool_shift(part, pool_count, r) for r in range(1, pool_count)]
        return shares[n]

    def serve(n, *first):
        block = after(come[n - 2], *first) if first else come[n - 2]
        if n - 2 in (3, 4):
            whole = shape((out_weight.shape[0] + kv_rows * pool_count, width), BF16)
            block = call(widen_kernel, "widen", whole, [meta, block, *shares[n - 2]])
        come[n] = ring_step(block, seq_count)
        return come[n]

    def arrivals(g):
        if g == 0:
            return [come[-1]]
        if g == steps:
            return [come[last]]
        return [come[2 * g - 1], come[2 * g]]

    def kv_of(g):
        if g == 0:
            return [kv_weight]
        if g < 3:
            return [part for n in (2 * g - 1, 2 * g) for part in shares[n]]
        return arrivals(g)

    serve(1)

    by_share = pl.BlockSpec((rows, share * HD), lambda g: (0, g))
    cumul, update = pl.pallas_call(
        update_kernel,
        name="update",
        grid=(INNER,),
        out_shape=[shape((INNER, share, rows), F32), shape((heads, HD + TAG, HD), BF16)],
        in_specs=[by_share, by_share, pl.BlockSpec((heads, rows), lambda g: (0, 0))],
        out_specs=[
            pl.BlockSpec((INNER, share, rows), lambda g: (0, 0, 0)),
            pl.BlockSpec((share, HD + TAG, HD), lambda g: (g, 0, 0)),
        ],
        cost_estimate=LIGHT,
        compiler_params=params(12),
    )(in_hbm(key_rows), in_hbm(value_rows), log_decay)
    update = after(update, come[0])
    update_other = seq_xor(update, seq_count, 1)
    serve(2, update_other)
    chip = call(
        chip_kernel, "chip_state", shape(update.shape, BF16), [meta, update, update_other]
    )
    chip_other = to_other_row(chip, seq_count, 0)
    inners = [inner_part(0, INNER // 2, query_rows, key_rows, value_rows, cumul)]
    chip_other = after(chip_other, inners[0], come[1])
    tagged = (heads // 2, HD + TAG, HD)
    plane_update = call(plane_kernel, "plane_state", shape(tagged, BF16), [meta, chip, chip_other])
    serve(3, plane_update)
    spread(1, plane_update)
    table = after(block_table, plane_update)
    tables = [block_table] + [pool_shift(table, pool_count, r) for r in range(1, pool_count)]
    total = plane_update
    before = []
    reach = 1
    while reach < planes:
        received = to_later_planes(total, seq_count, reach)
        if len(inners) < 3:
            query = after(query_rows, total)
            inners.append(
                inner_part(1 + len(inners), 1, query, key_rows, value_rows, cumul)
            )
            first = (come[2], *shares[1], *tables) if reach == 1 else (*shares[3], *shares[2])
            received[0] = after(received[0], inners[-1], *first)
        final = 2 * reach >= planes
        prefix, *rest = call(
            functools.partial(scan_kernel, reach),
            "scan_state",
            [shape(tagged, BF16)] * (1 if final else 2),
            [meta, *received, *before, plane_update],
        )
        if reach == 1:
            serve(4, prefix)
            spread(2, prefix)
            spread(3, prefix)
        before, total = [prefix], (rest or [None])[0]
        reach *= 2
    prefix_other = to_other_row(prefix, seq_count, 1)
    residual_other = seq_xor(after(residual, prefix), seq_count, 1)
    serve(5, prefix)
    own_state, away_state = call(
        start_kernel,
        "start_state",
        [shape((heads, HD, HD), BF16)] * 2,
        [meta, update, update_other, chip_other, prefix, prefix_other],
    )
    other_state = seq_xor(away_state, seq_count, 1)
    spread(4, own_state)
    other_state = after(other_state, come[4])

    mixed = pl.pallas_call(
        mixed_kernel,
        name="mixed",
        grid=(INNER,),
        out_shape=[shape((rows_here, wide), BF16)] * pool_count,
        in_specs=[SMEM, by_share]
        + [VMEM] * 3
        + [pl.BlockSpec((1, share, rows), lambda g: (g, 0, 0))]
        + [pl.BlockSpec((share, HD, HD), lambda g: (g, 0, 0))] * 2,
        out_specs=[pl.BlockSpec((rows_here, share * HD), lambda g: (0, g))] * pool_count,
        scratch_shapes=[pltpu.VMEM((rows, share * HD), F32)],
        cost_estimate=LIGHT,
        compiler_params=params(12),
    )(meta, in_hbm(query_rows), *inners, cumul, own_state, other_state)
    mixed_other = [seq_xor(part, seq_count, 1) for part in mixed]
    both = []

    def project(g, *first):
        blocks = arrivals(g)
        count = len(blocks)
        out_wide = count * width
        joins = not both
        sources = [after(both[0], *first)] if both else [*mixed, *mixed_other]
        joined = [shape((pool_count, chip_rows, wide), BF16)] if joins else []
        mine, *away = call(
            functools.partial(project_kernel, pool_count if joins else 0, count),
            "project",
            [shape((chip_rows, out_wide), F32)]
            + [shape((chip_rows, out_wide), BF16)] * (pool_count - 1)
            + joined,
            [*sources, *blocks],
            mib=12,
        )
        if joins:
            both.append(away.pop())
        arrived = [pool_shift(away[r - 1], pool_count, r) for r in range(1, pool_count)]
        return mine, arrived

    def cache(g, projected, sums, *first):
        mine, arrived = projected
        kv = kv_of(g)
        count = len(starts[g])
        out_wide = count * width
        around = [residual, residual_other, norm_gain.reshape(1, -1)]
        if width % HD:
            around = [
                jnp.concatenate([lax.dynamic_slice_in_dim(a, s, width, 1) for s in starts[g]], 1)
                for a in around
            ]
        return call(
            functools.partial(
                cache_kernel,
                not sums,
                count,
                pool_count,
                len(kv),
                width,
                3 + sum(len(x) for x in starts[:g]),
            ),
            "cache",
            [
                shape((rows_here, cache_width), F32),
                shape((rows_here, cache_width), BF16 if g == steps else F32),
            ]
            + [shape((rows_here, HD), F32)] * 2,
            [
                meta,
                after(mine, *first),
                *around,
                *kv,
                *arrived,
                *sums,
            ],
            [
                pltpu.VMEM((out_wide, cache_width), BF16),
                pltpu.VMEM((chip_rows, out_wide), BF16),
                pltpu.VMEM((chip_rows, out_wide), BF16),
                pltpu.SemaphoreType.DMA((2 * count,)),
            ],
            mib=12,
            far=() if width % HD else (2, 3),
        )

    projected = {0: project(0)}
    done = (projected[0][0],)
    sums = ()
    cached = 0

    def reduce_one():
        nonlocal sums, done, cached
        sums = cache(cached, projected[cached], sums, *done)
        done = (sums[2],)
        cached += 1

    for g in range(1, steps + 1):
        if g > 2:
            done = (*done, *[come[m] for m in (2 * g - 1, 2 * g) if m <= last])
        projected[g] = project(g, *done)
        done = (projected[g][0],)
        if g == 1:
            serve(6)
            continue
        if g == 2:
            done = (*done, residual_other)
            reduce_one()
            reduce_one()
        for n in (2 * g + 3, 2 * g + 4):
            if n not in come and n <= last:
                serve(n)
        while g < steps and cached <= g - 1:
            reduce_one()
    while cached <= steps:
        reduce_one()
    own_total, other_total, own_square, other_square = sums
    cache_rows = call(
        functools.partial(finish_kernel, width * seq_count),
        "finish",
        shape((rows_here, cache_width), BF16),
        [
            own_total,
            own_square,
            seq_xor(other_total, seq_count, 1),
            seq_xor(other_square, seq_count, 1),
        ],
    )
    pages = [cache_rows] + [pool_shift(cache_rows, pool_count, r) for r in range(1, pool_count)]
    page_cache = call(
        functools.partial(place_kernel, pool_count),
        "place",
        shape((slot_count, PAGE, cache_width), BF16),
        [meta, *tables, *pages],
    )
    return page_cache.reshape(1, 1, slot_count, PAGE, cache_width)


def solution(mesh):
    placed = (
        P("seq", "pool"),
        P("seq", "pool"),
        P("seq", "pool"),
        P("pool", "seq"),
        P(("seq", "pool"), None),
        P("pool", "seq"),
        P(),
        P("seq", None),
        P(("seq", "pool"), None),
    )
    return jax.shard_map(
        on_device,
        mesh=mesh,
        in_specs=placed,
        out_specs=P("seq", "pool", None, None, None),
        check_vma=False,
    )
```
